32 devices in a mesh: space: 16 (over z, y, core), chaos: 2 (over x).
Axes of the slice: x: 2, y: 2, z: 4, core: 2. Of those that a mesh axis runs over, the one named last changes fastest.
Arguments:
- right_side: float32 [168, 8192], P('chaos', 'space'), may hold values from -8 to 8, as said below
- diagonal: float32 [168, 8192], P('chaos', 'space'), may hold values from 1.5 to 4
- stiffness: float32 [9, 128, 64, 256], P(None, 'space'), may hold values from -0.015625 to 0.015625
- columns: int32 [128, 4], P('space'), may hold values from 0 to 9, as said below
- interface: int32 [16, 2], P('space'), may hold values from 0 to 7
- triples: int32 [885, 3], replicated, may hold values from 0 to 164, as said below
- coupling_values: float32 [885], replicated, may hold values from -1 to 1, as said below
Outputs:
- solution_field: float32 [168, 8192], P('chaos', 'space')
- residual: float32 [168, 8192], P('chaos', 'space')
The draws below stay inside these ranges and needn't reach their ends.
Inputs may be any that keep to these rules, and one draw needn't show every extreme that they name: `right_side`: mode slots 165 and beyond are zero in every row. `columns`: entry 0 of block row b is b mod 8. Values below 8 name the partition's own block rows, 8 to 8 the blocks received from the previous partition, the rest those from the next. `triples`: no triple repeats. Term 0 holds (0, i, i) once for every mode i below 165. Every other entry has a term t of 1 to 8 and comes with its mirror (t, j, i), i != j; each mode is the row mode of at most two entries of one such term. `coupling_values`: an entry and its mirror carry equal values, so every coupling[t] is symmetric.
All inputs are finite; a program needn't handle non-finite values.
Results may differ from the reference program's by a relative error of at most 0.0003.
Values sent between devices are 32-bit elements; how exact they have to be, the bound alone decides.
A program may use at most 64 MiB of HBM per device.

```python
import jax
import jax.numpy as jnp
import numpy as np
from jax import lax

MODES = 165
MODE_SLOTS = 168
TERMS = 9
BLOCK = 64
NNZ = 4
IFACE = 1
ITERS = 3
NBR = 8
PARTITIONS = 16
BLOCK_ROWS = 128
ROWS = 8192
N_SPACE = 16


def compositions(total, variables):
    if variables == 1:
        return [(total,)]
    result = []
    for first in range(total, -1, -1):
        for rest in compositions(total - first, variables - 1):
            result.append((first,) + rest)
    return result


def chaos_pattern():
    variables = TERMS - 1
    indices = []
    degree = 0
    while len(indices) < MODES:
        indices.extend(compositions(degree, variables))
        degree = degree + 1
    indices = indices[:MODES]
    lookup = {}
    for place in range(len(indices)):
        lookup[indices[place]] = place
    pair_terms = []
    pair_rows = []
    pair_cols = []
    for place in range(len(indices)):
        alpha = indices[place]
        for which in range(variables):
            raised = tuple((alpha[v] + (1 if v == which else 0) for v in range(variables)))
            if raised in lookup:
                pair_terms.append(which + 1)
                pair_rows.append(place)
                pair_cols.append(lookup[raised])
    return (np.array(pair_terms, np.int32), np.array(pair_rows, np.int32), np.array(pair_cols, np.int32))


def draw_right_side(key, part):
    keys = jax.random.split(key, 3)
    base = jax.random.normal(keys[0], (MODE_SLOTS, ROWS), jnp.float32)
    places = jnp.arange(ROWS, dtype=jnp.float32) / ROWS
    ramp = 1.0 + 2.0 * places
    vector = base
    vector = jnp.clip(vector * ramp[None, :], -8.0, 8.0)
    live = jnp.arange(MODE_SLOTS) < MODES
    return jnp.where(live[:, None], vector, 0.0).astype(jnp.float32)


def draw_columns(key, part):
    others = jax.random.randint(key, (BLOCK_ROWS, NNZ - 1), 0, NBR + 2 * IFACE)
    own = (jnp.arange(BLOCK_ROWS, dtype=jnp.int32) % NBR)[:, None]
    table = jnp.concatenate([own, others.astype(jnp.int32)], 1)
    return table.at[0, 1].set(NBR + 2 * IFACE - 1).astype(jnp.int32)


def draw_triples(key, part):
    pair_terms, pair_rows, pair_cols = chaos_pattern()
    relabel = jax.random.permutation(jax.random.fold_in(key, 11), MODES).astype(jnp.int32)
    own_modes = relabel[jnp.arange(MODES, dtype=jnp.int32)]
    diag_rows = jnp.stack([jnp.zeros((MODES,), jnp.int32), own_modes, own_modes], 1)
    terms = jnp.asarray(pair_terms)
    lower = relabel[jnp.asarray(pair_rows)]
    upper = relabel[jnp.asarray(pair_cols)]
    forward = jnp.stack([terms, lower, upper], 1)
    mirror = jnp.stack([terms, upper, lower], 1)
    return jnp.concatenate([diag_rows, forward, mirror], 0).astype(jnp.int32)


def draw_coupling_values(key, part):
    pair_terms, pair_rows, pair_cols = chaos_pattern()
    count = pair_terms.shape[0]
    diag_values = jax.random.uniform(jax.random.fold_in(key, 12), (MODES,), jnp.float32, -1.0, 1.0)
    pair_values = jax.random.uniform(jax.random.fold_in(key, 13), (count,), jnp.float32, -1.0, 1.0)
    return jnp.concatenate([diag_values, pair_values, pair_values], 0).astype(jnp.float32)


def touch_ends(drawn, own_key, low, largest):
    dims = drawn.shape
    spot = [jax.random.randint(jax.random.fold_in(own_key, axis), (), 0, dims[axis]) for axis in range(len(dims))]
    drawn = drawn.at[tuple(spot)].set(low)
    longest = dims.index(max(dims))
    spot[longest] = (spot[longest] + 1) % dims[longest]
    return drawn.at[tuple(spot)].set(largest)


def level_of(key, dims, shards, smallest, high):
    def one(dim, parts):
        draws = jax.random.uniform(jax.random.fold_in(jax.random.fold_in(key, 6), dim), (parts,), jnp.float32, smallest / len(shards), high / len(shards))
        return jnp.repeat(jnp.exp(draws), dims[dim] // parts).reshape((-1,) + (1,) * (len(dims) - dim - 1))

    gain = one(*shards[0])
    for cut in shards[1:]:
        gain = gain * one(*cut)
    return gain


def setup_inputs(seed: int = 0) -> dict:
    streams_of = jax.random.split(jax.random.key(seed), 8)
    right_side = draw_right_side(jax.random.fold_in(streams_of[7], 71), 0)
    diagonal = jnp.clip(1.5 + 2.5 * jax.random.uniform(streams_of[1], (MODE_SLOTS, ROWS), jnp.float32) ** level_of(streams_of[1], (MODE_SLOTS, ROWS), ((0, 2), (1, 16)), -0.2, 0.2), 1.5, 4.0)
    stiffness = jnp.clip(jax.random.uniform(streams_of[2], (TERMS, BLOCK_ROWS, BLOCK, NNZ * BLOCK), jnp.float32, -0.015625, 0.015625) * level_of(streams_of[2], (TERMS, BLOCK_ROWS, BLOCK, NNZ * BLOCK), ((1, 16),), -0.4, 0.0), -0.015625, 0.015625)
    columns = draw_columns(jax.random.fold_in(streams_of[7], 71), 0)
    interface = touch_ends(jax.random.randint(streams_of[4], (PARTITIONS, 2 * IFACE), 0, NBR), jax.random.fold_in(streams_of[4], 1), 0, NBR - 1).astype(jnp.int32)
    triples = draw_triples(jax.random.fold_in(streams_of[7], 71), 0)
    coupling_values = draw_coupling_values(jax.random.fold_in(streams_of[7], 71), 0)
    return {"right_side": right_side, "diagonal": diagonal, "stiffness": stiffness, "columns": columns, "interface": interface, "triples": triples, "coupling_values": coupling_values}


def coupling_table(triples, coupling_values):
    table = jnp.zeros((TERMS, MODE_SLOTS, MODE_SLOTS), jnp.float32)
    return table.at[triples[:, 0], triples[:, 1], triples[:, 2]].add(coupling_values)


def operate(vector, diagonal, stiffness, columns, interface, coupling):
    blocks = vector.reshape(MODE_SLOTS, N_SPACE, NBR, BLOCK)
    owners = jnp.arange(N_SPACE, dtype=jnp.int32)[:, None]
    outgoing = blocks[:, owners, interface, :]
    zeros_rim = jnp.zeros((MODE_SLOTS, 1, IFACE, BLOCK), jnp.float32)
    from_left = jnp.concatenate([zeros_rim, outgoing[:, :-1, IFACE:]], 1)
    from_right = jnp.concatenate([outgoing[:, 1:, :IFACE], zeros_rim], 1)
    extended = jnp.concatenate([blocks, from_left, from_right], 2)
    col_index = columns.reshape(N_SPACE, NBR * NNZ).astype(jnp.int32)
    picked = jnp.take_along_axis(extended, col_index[None, :, :, None], axis=2)
    picked = picked.reshape(MODE_SLOTS, N_SPACE, NBR, NNZ * BLOCK)
    matrices = stiffness.reshape(TERMS, N_SPACE, NBR, BLOCK, NNZ * BLOCK)
    spatial = jnp.einsum('msbk,tsbck->tmsbc', picked, matrices, precision=lax.Precision.HIGHEST)
    spatial = spatial.reshape(TERMS, MODE_SLOTS, ROWS)
    coupled = jnp.einsum('tij,tjr->ir', coupling, spatial, precision=lax.Precision.HIGHEST)
    return diagonal * vector + coupled


def reference(right_side, diagonal, stiffness, columns, interface, triples, coupling_values):
    coupling = coupling_table(triples, coupling_values)
    solution_field = jnp.zeros_like(right_side)
    residual, direction = right_side, right_side
    norm_now = jnp.sum(residual * residual)
    for iteration in range(ITERS):
        applied = operate(direction, diagonal, stiffness, columns, interface, coupling)
        step_size = norm_now / jnp.sum(direction * applied)
        solution_field = solution_field + step_size * direction
        residual = residual - step_size * applied
        norm_next = jnp.sum(residual * residual)
        direction = residual + (norm_next / norm_now) * direction
        norm_now = norm_next
    return solution_field, residual
```

```python
import functools

import jax
import jax.numpy as jnp
from jax import lax
from jax.experimental import pallas as pl
from jax.experimental.pallas import tpu as pltpu
from jax.sharding import PartitionSpec as P

MESH = pl.DeviceIdType.MESH
ITERS = 3
LANES = 128
SHIFT = 2.75
GAMMA = (0.0, 0.52083333, 0.41666667)
PAIRS = ((0, 0), (0, 1), (1, 1), (0, 2), (1, 2), (2, 2), (0, 3), (1, 3), (2, 3))


def split(x):
    hi = x.astype(jnp.bfloat16)
    lo = (x - hi.astype(jnp.float32)).astype(jnp.bfloat16)
    return hi, lo


def dot_nt(a, b):
    return lax.dot_general(a, b, (((1,), (1,)), ((), ())), preferred_element_type=jnp.float32)


def dot_nn(a, b):
    return lax.dot_general(a, b, (((1,), (0,)), ((), ())), preferred_element_type=jnp.float32)


def low_half(shape):
    return lax.broadcasted_iota(jnp.int32, shape, len(shape) - 1) < LANES // 2


def swap(x):
    return pltpu.roll(x, LANES // 2, 1)


def packed_rows(rows):
    return (rows // 8 + 1) // 2 * 8


def pack(x):
    rows = x.shape[0]
    part = packed_rows(rows)
    return jnp.where(low_half((part, LANES)), x[:part], x[rows - part :])


def unpack(x, rows):
    part = x.shape[0]
    turned = swap(x)
    low = low_half(x.shape)
    top = jnp.where(low, x, turned)
    bottom = jnp.where(low, turned, x)
    return jnp.concatenate([top, bottom[2 * part - rows :]], 0)


def one_way(x):
    return jnp.where(x, 1, 0)


def kernel(
    n_space, n_chaos, stage,
    b_ref, d_ref, k_hbm, col_ref, if_ref, tri_ref, val_ref,
    x_out, r_out,
    kf, khi, klo, c2, cdiag, gb, gd, nat, ef, vec, dg, rodd, reven,
    own_send, halo0, halo_out, halo_in, stat, red1, red2, natv,
    k_sem, gb_send, gb_recv, gd_send, gd_recv, h0_send, h0_recv, h_send, h_recv,
    r1_send, r1_recv, r2_send, r2_recv,
):
    f32 = jnp.float32
    modes, width = b_ref.shape
    hp = gb.shape[1]
    mp = n_chaos * hp
    terms, nbr, block, _ = kf.shape
    nnz = col_ref.shape[0]
    pairs = nbr // 2
    even_terms = (terms - 1) // 2
    s = lax.axis_index("space")
    c = lax.axis_index("chaos")

    k_copy = pltpu.make_async_copy(k_hbm, kf, k_sem)
    k_copy.start()

    barrier = pltpu.get_barrier_semaphore()
    group, place = s // stage, s % stage
    n_group = n_space // stage
    has_left, has_right = s > 0, s < n_space - 1

    def greet(space, chaos):
        pl.semaphore_signal(barrier, inc=1, device_id=(space, chaos), device_id_type=MESH)

    for d in range(1, n_chaos):
        greet(s, (c + d) % n_chaos)
    for d in range(n_chaos):
        @pl.when(has_left)
        def _():
            greet(s - 1, (c + d) % n_chaos)

        @pl.when(has_right)
        def _():
            greet(s + 1, (c + d) % n_chaos)
    for d in range(1, stage):
        greet(group * stage + (place + d) % stage, c)
    for d in range(1, n_group):
        greet(((group + d) % n_group) * stage + place, c)

    own_b = jnp.concatenate([b_ref[...], jnp.zeros((hp - modes, width), f32)], 0) if hp > modes else b_ref[...]
    own_d = jnp.concatenate([d_ref[...], jnp.zeros((hp - modes, width), f32)], 0) if hp > modes else d_ref[...]
    gb[c] = own_b
    gd[c] = own_d
    low_hp = low_half((hp, LANES))
    for q in range(pairs):
        chunk = own_b[:, q * LANES : (q + 1) * LANES]
        turned = swap(chunk)
        natv[0, 2 * q] = jnp.where(low_hp, chunk, turned)
        natv[0, 2 * q + 1] = jnp.where(low_hp, turned, chunk)
    if0, if1 = if_ref[0, 0], if_ref[0, 1]
    own_send[1] = pack(natv[0, if0])
    own_send[0] = pack(natv[0, if1])

    pl.semaphore_wait(
        barrier,
        (n_chaos - 1) + n_chaos * (one_way(has_left) + one_way(has_right)) + (stage - 1) + (n_group - 1),
    )

    def halo0_copy(side, d):
        return pltpu.make_async_remote_copy(
            src_ref=own_send.at[side], dst_ref=halo0.at[side, c],
            send_sem=h0_send.at[side, d], recv_sem=h0_recv.at[side, d],
            device_id=(s + 1 if side == 0 else s - 1, (c + d) % n_chaos), device_id_type=MESH,
        )

    def gather_copy(buf, send, recv, d):
        return pltpu.make_async_remote_copy(
            src_ref=buf.at[c], dst_ref=buf.at[c], send_sem=send.at[d], recv_sem=recv.at[d],
            device_id=(s, (c + d) % n_chaos), device_id_type=MESH,
        )

    for d in range(n_chaos):
        @pl.when(has_right)
        def _():
            halo0_copy(0, d).start()

        @pl.when(has_left)
        def _():
            halo0_copy(1, d).start()
    for d in range(1, n_chaos):
        gather_copy(gb, gb_send, gb_recv, d).start()
    for d in range(1, n_chaos):
        gather_copy(gd, gd_send, gd_recv, d).start()

    second = jnp.where(if1 == if0, jnp.where(if0 == 0, 1, 0), if1)
    small, large = jnp.minimum(if0, second), jnp.maximum(if0, second)

    def block_at(k):
        if isinstance(k, int) and k < 2:
            return if0 if k == 0 else second
        row = k - 2
        row = row + one_way(row >= small)
        return row + one_way(row >= large)

    def place_of(row):
        rest = 2 + row - one_way(if0 < row) - one_way(second < row)
        found = jnp.where(row == if0, 0, jnp.where(row == second, 1, rest))
        return jnp.where(row >= nbr, row, found)

    def slot(mode):
        shift = jnp.zeros_like(mode)
        for h in range(1, n_chaos):
            shift = shift + one_way(mode >= h * modes)
        return mode + (hp - modes) * shift

    entries = tri_ref.shape[1]
    term = tri_ref[0:1, :]
    row = slot(tri_ref[1:2, :])
    col = slot(tri_ref[2:3, :])
    values = val_ref[...]
    hit = lax.broadcasted_iota(jnp.int32, (mp, entries), 0) == row
    spread = jnp.where(hit, values, 0.0)
    cdiag[...] = jnp.broadcast_to(
        jnp.sum(jnp.where(term == 0, spread, 0.0), axis=1, keepdims=True), (mp, LANES)
    )
    spread_hi, spread_lo = split(spread)
    spread2 = jnp.concatenate([spread_hi, spread_lo], 0)
    rows_iota = lax.broadcasted_iota(jnp.int32, (even_terms * mp, entries), 0)
    for parity in range(2):
        first = 1 if parity == 0 else 2
        mine = (term > 0) & (term % 2 == first % 2)
        key = jnp.where(mine, ((term - first) // 2) * mp + col, -1)
        hot = jnp.where(rows_iota == key, 1.0, 0.0).astype(jnp.bfloat16)
        c2[parity] = dot_nt(spread2, hot).astype(jnp.bfloat16)

    k_copy.wait()

    def prepare(j, _):
        for odd in range(2):
            k = 2 * j + odd
            source = jnp.where(k == 0, if0, jnp.where(k == 1, second, block_at(k)))
            for t in range(terms):
                hi, lo = split(kf[t, source])
                if t == 0:
                    at = [even_terms * LANES, even_terms * LANES + block]
                else:
                    tau, late = (t - 1) // 2, (t - 1) % 2
                    at = [tau * LANES + (late ^ odd) * block]
                for a in at:
                    khi[k, a : a + block, :] = hi
                    klo[k, a : a + block, :] = lo
        return 0

    lax.fori_loop(0, pairs, prepare, 0)

    low = low_half((mp, LANES))

    def spread_blocks(buf):
        for q in range(pairs):
            for h in range(n_chaos):
                chunk = buf[h, :, q * LANES : (q + 1) * LANES]
                turned = swap(chunk)
                nat[2 * q, h * hp : (h + 1) * hp] = jnp.where(low_hp, chunk, turned)
                nat[2 * q + 1, h * hp : (h + 1) * hp] = jnp.where(low_hp, turned, chunk)

    for d in range(1, n_chaos):
        gather_copy(gb, gb_send, gb_recv, d).wait()
    spread_blocks(gb)
    for p in range(pairs):
        one, two = nat[block_at(2 * p)], nat[block_at(2 * p + 1)]
        ef[0, 2 * p] = one
        ef[0, 2 * p + 1] = two
        vec[0, p] = jnp.where(low, one, two)

    def fill(side, now, read):
        present = has_left if side == 0 else has_right

        @pl.when(present)
        def _():
            read()

        @pl.when(jnp.logical_not(present))
        def _():
            ef[now, nbr + side] = jnp.zeros((mp, LANES), f32)

    for side in range(2):
        def read_first():
            for d in range(n_chaos):
                halo0_copy(side, d).wait_recv()
            for h in range(n_chaos):
                ef[0, nbr + side, h * hp : (h + 1) * hp] = unpack(halo0[side, h], hp)

        fill(side, 0, read_first)
    for side in range(2):
        @pl.when(has_right if side == 0 else has_left)
        def _():
            for d in range(n_chaos):
                halo0_copy(side, d).wait_send()

    def halo_copy(it, side):
        return pltpu.make_async_remote_copy(
            src_ref=halo_out.at[it, side], dst_ref=halo_in.at[it, side],
            send_sem=h_send.at[it, side], recv_sem=h_recv.at[it, side],
            device_id=(s + 1 if side == 0 else s - 1, c), device_id_type=MESH,
        )

    places = [[place_of(col_ref[n, block_at(k)]) for n in range(nnz)] for k in range(nbr)]
    right_place = place_of(if1)
    sums = {}

    def add_product(i, j, one, two):
        part = jnp.sum((one * two).reshape(mp // 8, 8, LANES), axis=0)
        sums[(i, j)] = sums[(i, j)] + part if (i, j) in sums else part

    for p in range(pairs):
        add_product(0, 0, vec[0, p], vec[0, p])

    scale0 = cdiag[...]
    half_pairs = pairs // 2
    n_odd = even_terms * LANES
    for it in range(ITERS):
        now, later = it % 2, (it + 1) % 2
        for half in range(2):
            zeros = []
            for step in range(half_pairs):
                p = half * half_pairs + step
                made = []
                for odd in range(2):
                    k = 2 * p + odd
                    at = places[k]
                    picked = jnp.concatenate(
                        [
                            jnp.where(low, ef[now, at[2 * m]], ef[now, at[2 * m + 1]])
                            for m in range(nnz // 2)
                        ],
                        1,
                    )
                    hi, lo = split(picked)
                    both = dot_nt(jnp.concatenate([hi, lo], 0), khi[k])
                    made.append(both[:mp] + both[mp:] + dot_nt(hi, klo[k]))
                first, next_ = made
                to = pl.ds(step * LANES, LANES)
                for tau in range(even_terms):
                    a = first[:, tau * LANES : (tau + 1) * LANES]
                    b = next_[:, tau * LANES : (tau + 1) * LANES]
                    hi, lo = split(jnp.where(low, a, b))
                    rodd[0, tau * mp : (tau + 1) * mp, to] = hi
                    rodd[1, tau * mp : (tau + 1) * mp, to] = lo
                    hi, lo = split(jnp.where(low, b, a))
                    reven[0, tau * mp : (tau + 1) * mp, to] = hi
                    reven[1, tau * mp : (tau + 1) * mp, to] = lo
                zeros.append(jnp.where(low, first[:, n_odd:], next_[:, n_odd:]))
            coupled = []
            for parity, rhs in ((0, rodd), (1, reven)):
                both = dot_nn(c2[parity], rhs[0])
                coupled.append(both[:mp] + both[mp:] + dot_nn(c2[parity, :mp], rhs[1]))
            if it == 0 and half == 0:
                for d in range(1, n_chaos):
                    gather_copy(gd, gd_send, gd_recv, d).wait()
                spread_blocks(gd)
                for p in range(pairs):
                    one, two = nat[block_at(2 * p)], nat[block_at(2 * p + 1)]
                    dg[p] = jnp.where(low, one, two) - SHIFT
            for step in range(half_pairs):
                p = half * half_pairs + step
                at = slice(step * LANES, (step + 1) * LANES)
                new = coupled[0][:, at] + swap(coupled[1][:, at]) + scale0 * zeros[step]
                new = dg[p] * vec[it, p] + new
                if it > 0:
                    new = new - GAMMA[it] * vec[it - 1, p]
                vec[it + 1, p] = new
                for j in range(it + 1):
                    add_product(j, it + 1, vec[j, p], new)
                if it < ITERS - 1:
                    add_product(it + 1, it + 1, new, new)
                    turned = swap(new)
                    ef[later, 2 * p] = jnp.where(low, new, turned)
                    ef[later, 2 * p + 1] = jnp.where(low, turned, new)
            if it < ITERS - 1 and half == 0:
                halo_out[it, 1] = pack(ef[later, 0])
                halo_out[it, 0] = pack(ef[later, right_place])

                @pl.when(has_right)
                def _():
                    halo_copy(it, 0).start()

                @pl.when(has_left)
                def _():
                    halo_copy(it, 1).start()
        if it < ITERS - 1:
            for side in range(2):
                def read_next():
                    halo_copy(it, side).wait_recv()
                    ef[later, nbr + side] = unpack(halo_in[it, side], mp)

                fill(side, later, read_next)
            for side in range(2):
                @pl.when(has_right if side == 0 else has_left)
                def _():
                    halo_copy(it, side).wait_send()

    stat[...] = jnp.zeros_like(stat)
    for e, pair in enumerate(PAIRS):
        stat[e : e + 1, :] = jnp.sum(sums[pair], axis=0, keepdims=True)

    def reduce_copy(level, d):
        if level == 0:
            target, src, dst, send, recv = group * stage + (place + d) % stage, stat, red1.at[place], r1_send, r1_recv
        else:
            target, src, dst, send, recv = ((group + d) % n_group) * stage + place, stat, red2.at[group], r2_send, r2_recv
        return pltpu.make_async_remote_copy(
            src_ref=src, dst_ref=dst, send_sem=send.at[d], recv_sem=recv.at[d],
            device_id=(target, c), device_id_type=MESH,
        )

    red1[place] = stat[...]
    for d in range(1, stage):
        reduce_copy(0, d).start()

    mine = pl.ds(pl.multiple_of(c * hp, 8), hp)
    back = [place_of(jnp.int32(k)) for k in range(nbr)]
    for j in range(ITERS + 1):
        for p in range(pairs):
            chunk = vec[j, p, mine, :]
            turned = swap(chunk)
            natv[j, 2 * p] = jnp.where(low_hp, chunk, turned)
            natv[j, 2 * p + 1] = jnp.where(low_hp, turned, chunk)

    for d in range(1, stage):
        reduce_copy(0, d).wait()
    total = red1[0]
    for g in range(1, stage):
        total = total + red1[g]
    stat[...] = total
    red2[group] = total
    for d in range(1, n_group):
        reduce_copy(1, d).start()
    for d in range(1, n_group):
        reduce_copy(1, d).wait()
    total = red2[0]
    for g in range(1, n_group):
        total = total + red2[g]
    total = jnp.sum(total, axis=1, keepdims=True)
    gram = {}
    for e, (i, j) in enumerate(PAIRS):
        gram[(i, j)] = gram[(j, i)] = total[e : e + 1, :]

    def inner(one, two):
        value = None
        for i, a in one.items():
            for j, b in two.items():
                part = a * b * gram[(i, j)]
                value = part if value is None else value + part
        return value

    def plus(one, scale, two):
        result = dict(one)
        for i, a in two.items():
            result[i] = result[i] + scale * a if i in result else scale * a
        return result

    def image_of(vector):
        result = {}
        for k, a in vector.items():
            result = plus(result, a, {k: jnp.full((1, 1), SHIFT, f32), k + 1: jnp.ones((1, 1), f32)})
            if k > 0:
                result = plus(result, a, {k - 1: jnp.full((1, 1), GAMMA[k], f32)})
        return result

    residual = {0: jnp.ones((1, 1), f32)}
    direction = dict(residual)
    field = {}
    norm_now = gram[(0, 0)]
    for it in range(ITERS):
        image = image_of(direction)
        alpha = norm_now / inner(direction, image)
        field = plus(field, alpha, direction)
        residual = plus(residual, -alpha, image)
        if it < ITERS - 1:
            norm_next = inner(residual, residual)
            direction = plus(residual, norm_next / norm_now, direction)
            norm_now = norm_next

    for q in range(pairs):
        parts = []
        for j in range(ITERS + 1):
            parts.append(jnp.where(low_hp, natv[j, back[2 * q]], natv[j, back[2 * q + 1]]))
        for coefs, out in ((field, x_out), (residual, r_out)):
            value = None
            for j, a in coefs.items():
                part = a * parts[j]
                value = part if value is None else value + part
            out[:, q * LANES : (q + 1) * LANES] = value[:modes]


def per_device(right_side, diagonal, stiffness, columns, interface, triples, coupling_values):
    n_space, n_chaos = lax.axis_size("space"), lax.axis_size("chaos")
    modes, width = right_side.shape
    terms, nbr, block, depth = stiffness.shape
    hp = (modes + 7) // 8 * 8
    mp = n_chaos * hp
    pairs = nbr // 2
    even_terms = (terms - 1) // 2
    cols = even_terms * LANES + 2 * block
    stage = 1
    while stage * stage < n_space:
        stage *= 2
    n_group = n_space // stage
    f32, bf16 = jnp.float32, jnp.bfloat16
    vmem = pl.BlockSpec(memory_space=pltpu.VMEM)
    smem = pl.BlockSpec(memory_space=pltpu.SMEM)
    dma = pltpu.SemaphoreType.DMA
    out = jax.ShapeDtypeStruct((modes, width), f32)
    return pl.pallas_call(
        functools.partial(kernel, n_space, n_chaos, stage),
        out_shape=(out, out),
        in_specs=[vmem, vmem, pl.BlockSpec(memory_space=pl.ANY), smem, smem, vmem, vmem],
        out_specs=(vmem, vmem),
        scratch_shapes=[
            pltpu.VMEM(stiffness.shape, f32),
            pltpu.VMEM((nbr, cols, depth), bf16),
            pltpu.VMEM((nbr, cols, depth), bf16),
            pltpu.VMEM((2, 2 * mp, even_terms * mp), bf16),
            pltpu.VMEM((mp, LANES), f32),
            pltpu.VMEM((n_chaos, hp, width), f32),
            pltpu.VMEM((n_chaos, hp, width), f32),
            pltpu.VMEM((nbr, mp, LANES), f32),
            pltpu.VMEM((2, nbr + 2, mp, LANES), f32),
            pltpu.VMEM((ITERS + 1, pairs, mp, LANES), f32),
            pltpu.VMEM((pairs, mp, LANES), f32),
            pltpu.VMEM((2, even_terms * mp, pairs // 2 * LANES), bf16),
            pltpu.VMEM((2, even_terms * mp, pairs // 2 * LANES), bf16),
            pltpu.VMEM((2, packed_rows(hp), LANES), f32),
            pltpu.VMEM((2, n_chaos, packed_rows(hp), LANES), f32),
            pltpu.VMEM((ITERS - 1, 2, packed_rows(mp), LANES), f32),
            pltpu.VMEM((ITERS - 1, 2, packed_rows(mp), LANES), f32),
            pltpu.VMEM((16, LANES), f32),
            pltpu.VMEM((stage, 16, LANES), f32),
            pltpu.VMEM((n_group, 16, LANES), f32),
            pltpu.VMEM((ITERS + 1, nbr, hp, LANES), f32),
            dma,
            dma((n_chaos,)), dma((n_chaos,)), dma((n_chaos,)), dma((n_chaos,)),
            dma((2, n_chaos)), dma((2, n_chaos)),
            dma((ITERS - 1, 2)), dma((ITERS - 1, 2)),
            dma((stage,)), dma((stage,)), dma((n_group,)), dma((n_group,)),
        ],
        compiler_params=pltpu.CompilerParams(
            collective_id=0, has_side_effects=True, vmem_limit_bytes=56 * 1024 * 1024
        ),
        name="solve",
    )(
        right_side, diagonal, stiffness, columns.T, interface, triples.T,
        coupling_values.reshape(1, -1),
    )


def solution(mesh):
    placed = (
        P("chaos", "space"),
        P("chaos", "space"),
        P(None, "space", None, None),
        P("space", None),
        P("space", None),
        P(),
        P(),
    )
    return jax.shard_map(
        per_device,
        mesh=mesh,
        in_specs=placed,
        out_specs=(P("chaos", "space"), P("chaos", "space")),
        check_vma=False,
    )
```

```python
import functools

import jax
import jax.numpy as jnp
from jax import lax
from jax.experimental import pallas as pl
from jax.experimental.pallas import tpu as pltpu
from jax.sharding import PartitionSpec as P

MESH = pl.DeviceIdType.MESH
ITERS = 3
LANES = 128
SHIFT = 2.75
GAMMA = (0.0, 0.52083333, 0.41666667)
PAIRS = ((0, 0), (0, 1), (1, 1), (0, 2), (1, 2), (2, 2), (0, 3), (1, 3), (2, 3))


def split(x):
    hi = x.astype(jnp.bfloat16)
    lo = (x - hi.astype(jnp.float32)).astype(jnp.bfloat16)
    return hi, lo


def dot_nt(a, b):
    return lax.dot_general(a, b, (((1,), (1,)), ((), ())), preferred_element_type=jnp.float32)


def dot_nn(a, b):
    return lax.dot_general(a, b, (((1,), (0,)), ((), ())), preferred_element_type=jnp.float32)


def low_half(shape):
    return lax.broadcasted_iota(jnp.int32, shape, len(shape) - 1) < LANES // 2


def swap(x):
    return pltpu.roll(x, LANES // 2, 1)


def packed_rows(rows):
    return (rows // 8 + 1) // 2 * 8


def pack(x):
    rows = x.shape[0]
    part = packed_rows(rows)
    return jnp.where(low_half((part, LANES)), x[:part], x[rows - part :])


def unpack(x, rows):
    part = x.shape[0]
    turned = swap(x)
    low = low_half(x.shape)
    top = jnp.where(low, x, turned)
    bottom = jnp.where(low, turned, x)
    return jnp.concatenate([top, bottom[2 * part - rows :]], 0)


def one_way(x):
    return jnp.where(x, 1, 0)


def kernel(
    n_space, n_chaos, stage,
    b_ref, d_ref, k_hbm, col_ref, if_ref, tri_ref, val_ref,
    v0_out, v1_out, v2_out, v3_out, coef_out,
    kf, khi, klo, c3, cdiag, gb, gd, nat, ef0, ef1, vec, dg, picked, rodd, reven,
    own_send, own_blocks, halo0, halo_out, halo_in, stat, red1, red2, natv,
    k_sem, gb_send, gb_recv, gd_send, gd_recv, h0_send, h0_recv, h_send, h_recv,
    r1_send, r1_recv, r2_send, r2_recv,
):
    f32 = jnp.float32
    modes, width = b_ref.shape
    hp = gb.shape[1]
    mp = n_chaos * hp
    terms, nbr, block, _ = kf.shape
    nnz = col_ref.shape[0]
    pairs = nbr // 2
    even_terms = (terms - 1) // 2
    depth = rodd.shape[2]
    ef = (ef0, ef1)
    s = lax.axis_index("space")
    c = lax.axis_index("chaos")

    k_copy = pltpu.make_async_copy(k_hbm, kf, k_sem)
    k_copy.start()

    barrier = pltpu.get_barrier_semaphore()
    group, place = s // stage, s % stage
    n_group = n_space // stage
    has_left, has_right = s > 0, s < n_space - 1

    def greet(space, chaos):
        pl.semaphore_signal(barrier, inc=1, device_id=(space, chaos), device_id_type=MESH)

    for d in range(1, n_chaos):
        greet(s, (c + d) % n_chaos)
    for d in range(n_chaos):
        @pl.when(has_left)
        def _():
            greet(s - 1, (c + d) % n_chaos)

        @pl.when(has_right)
        def _():
            greet(s + 1, (c + d) % n_chaos)
    for d in range(1, stage):
        greet(group * stage + (place + d) % stage, c)
    for d in range(1, n_group):
        greet(((group + d) % n_group) * stage + place, c)

    own_b = jnp.concatenate([b_ref[...], jnp.zeros((hp - modes, width), f32)], 0) if hp > modes else b_ref[...]
    own_d = jnp.concatenate([d_ref[...], jnp.zeros((hp - modes, width), f32)], 0) if hp > modes else d_ref[...]
    gb[c] = own_b
    gd[c] = own_d
    low_hp = low_half((hp, LANES))
    for q in range(pairs):
        chunk = own_b[:, q * LANES : (q + 1) * LANES]
        turned = swap(chunk)
        own_blocks[2 * q] = jnp.where(low_hp, chunk, turned)
        own_blocks[2 * q + 1] = jnp.where(low_hp, turned, chunk)
    if0, if1 = if_ref[0, 0], if_ref[0, 1]
    own_send[1] = pack(own_blocks[if0])
    own_send[0] = pack(own_blocks[if1])

    pl.semaphore_wait(
        barrier,
        (n_chaos - 1) + n_chaos * (one_way(has_left) + one_way(has_right)) + (stage - 1) + (n_group - 1),
    )

    def halo0_copy(side, d):
        return pltpu.make_async_remote_copy(
            src_ref=own_send.at[side], dst_ref=halo0.at[side, c],
            send_sem=h0_send.at[side, d], recv_sem=h0_recv.at[side, d],
            device_id=(s + 1 if side == 0 else s - 1, (c + d) % n_chaos), device_id_type=MESH,
        )

    def gather_copy(buf, send, recv, d):
        return pltpu.make_async_remote_copy(
            src_ref=buf.at[c], dst_ref=buf.at[c], send_sem=send.at[d], recv_sem=recv.at[d],
            device_id=(s, (c + d) % n_chaos), device_id_type=MESH,
        )

    for d in range(n_chaos):
        @pl.when(has_right)
        def _():
            halo0_copy(0, d).start()

        @pl.when(has_left)
        def _():
            halo0_copy(1, d).start()
    for d in range(1, n_chaos):
        gather_copy(gb, gb_send, gb_recv, d).start()
    for d in range(1, n_chaos):
        gather_copy(gd, gd_send, gd_recv, d).start()

    second = jnp.where(if1 == if0, jnp.where(if0 == 0, 1, 0), if1)
    small, large = jnp.minimum(if0, second), jnp.maximum(if0, second)

    def block_at(k):
        if isinstance(k, int) and k < 2:
            return if0 if k == 0 else second
        row = k - 2
        row = row + one_way(row >= small)
        return row + one_way(row >= large)

    def place_of(row):
        rest = 2 + row - one_way(if0 < row) - one_way(second < row)
        found = jnp.where(row == if0, 0, jnp.where(row == second, 1, rest))
        return jnp.where(row >= nbr, row, found)

    def slot(mode):
        shift = jnp.zeros_like(mode)
        for h in range(1, n_chaos):
            shift = shift + one_way(mode >= h * modes)
        return mode + (hp - modes) * shift

    entries = tri_ref.shape[1]
    term = tri_ref[0:1, :]
    row = slot(tri_ref[1:2, :])
    col = slot(tri_ref[2:3, :])
    values = val_ref[...].reshape(1, entries)
    hit = lax.broadcasted_iota(jnp.int32, (mp, entries), 0) == row
    spread = jnp.where(hit, values, 0.0)
    cdiag[...] = jnp.broadcast_to(
        jnp.sum(jnp.where(term == 0, spread, 0.0), axis=1, keepdims=True), (mp, LANES)
    )
    spread_hi, spread_lo = split(spread)
    spread2 = jnp.concatenate([spread_hi, spread_lo], 0)
    rows_iota = lax.broadcasted_iota(jnp.int32, (depth, entries), 0)
    for parity in range(2):
        first = 1 if parity == 0 else 2
        mine = (term > 0) & (term % 2 == first % 2)
        key = jnp.where(mine, ((term - first) // 2) * mp + col, -1)
        hot = jnp.where(rows_iota == key, 1.0, 0.0).astype(jnp.bfloat16)
        both = dot_nt(spread2, hot).astype(jnp.bfloat16)
        c3[parity, :, :depth] = both[:mp]
        c3[parity, :, depth : 2 * depth] = both[mp:]
        c3[parity, :, 2 * depth :] = both[:mp]
    if depth > even_terms * mp:
        rest = jnp.zeros((depth - even_terms * mp, rodd.shape[3]), jnp.bfloat16)
        for half in range(2):
            for part in range(2):
                rodd[half, part, even_terms * mp :, :] = rest
                reven[half, part, even_terms * mp :, :] = rest

    k_copy.wait()

    def prepare(j, _):
        for odd in range(2):
            k = 2 * j + odd
            source = jnp.where(k == 0, if0, jnp.where(k == 1, second, block_at(k)))
            for t in range(terms):
                hi, lo = split(kf[t, source])
                if t == 0:
                    at = [even_terms * LANES, even_terms * LANES + block]
                else:
                    tau, late = (t - 1) // 2, (t - 1) % 2
                    at = [tau * LANES + (late ^ odd) * block]
                for a in at:
                    khi[k, a : a + block, :] = hi
                    klo[k, a : a + block, :] = lo
        return 0

    lax.fori_loop(0, pairs, prepare, 0)

    low = low_half((mp, LANES))

    def spread_blocks(buf):
        for q in range(pairs):
            for h in range(n_chaos):
                chunk = buf[h, :, q * LANES : (q + 1) * LANES]
                turned = swap(chunk)
                nat[2 * q, h * hp : (h + 1) * hp] = jnp.where(low_hp, chunk, turned)
                nat[2 * q + 1, h * hp : (h + 1) * hp] = jnp.where(low_hp, turned, chunk)

    for d in range(1, n_chaos):
        gather_copy(gb, gb_send, gb_recv, d).wait()
    spread_blocks(gb)
    for p in range(pairs):
        one, two = nat[block_at(2 * p)], nat[block_at(2 * p + 1)]
        ef0[2 * p] = one
        ef0[2 * p + 1] = two
        vec[0, p] = jnp.where(low, one, two)

    def fill(side, now, read):
        present = has_left if side == 0 else has_right

        @pl.when(present)
        def _():
            read()

        @pl.when(jnp.logical_not(present))
        def _():
            ef[now][nbr + side] = jnp.zeros((mp, LANES), f32)

    for side in range(2):
        def read_first():
            for d in range(n_chaos):
                halo0_copy(side, d).wait_recv()
            for h in range(n_chaos):
                ef0[nbr + side, h * hp : (h + 1) * hp] = unpack(halo0[side, h], hp)

        fill(side, 0, read_first)
    for side in range(2):
        @pl.when(has_right if side == 0 else has_left)
        def _():
            for d in range(n_chaos):
                halo0_copy(side, d).wait_send()

    def halo_copy(it, side):
        return pltpu.make_async_remote_copy(
            src_ref=halo_out.at[it, side], dst_ref=halo_in.at[it, side],
            send_sem=h_send.at[it, side], recv_sem=h_recv.at[it, side],
            device_id=(s + 1 if side == 0 else s - 1, c), device_id_type=MESH,
        )

    places = [[place_of(col_ref[n, block_at(k)]) for n in range(nnz)] for k in range(nbr)]
    right_place = place_of(if1)
    sums = {}

    def add_product(i, j, one, two):
        part = jnp.sum((one * two).reshape(mp // 8, 8, LANES), axis=0)
        sums[(i, j)] = sums[(i, j)] + part if (i, j) in sums else part

    for p in range(pairs):
        add_product(0, 0, vec[0, p], vec[0, p])

    scale0 = cdiag[...]
    half_pairs = pairs // 2
    n_odd = even_terms * LANES
    wide = nnz * block
    for it in range(ITERS):
        now, later = it % 2, (it + 1) % 2
        for half in range(2):
            zeros = []
            for step in range(half_pairs):
                p = half * half_pairs + step
                for k in (2 * p, 2 * p + 1):
                    at = places[k]
                    for m in range(nnz // 2):
                        hi, lo = split(jnp.where(low, ef[now][at[2 * m]], ef[now][at[2 * m + 1]]))
                        picked[k, :, m * LANES : (m + 1) * LANES] = hi
                        picked[k, :, wide + m * LANES : wide + (m + 1) * LANES] = lo
            for step in range(half_pairs):
                p = half * half_pairs + step
                to = pl.ds(step * LANES, LANES)
                for start in range(0, n_odd + 2 * block, 2 * LANES):
                    stop = min(start + 2 * LANES, n_odd + 2 * block)
                    made = []
                    for k in (2 * p, 2 * p + 1):
                        hi, lo = picked[k, :, :wide], picked[k, :, wide:]
                        k_hi, k_lo = khi[k, start:stop, :], klo[k, start:stop, :]
                        made.append(
                            dot_nt(jnp.concatenate([hi, lo, hi], 1), jnp.concatenate([k_hi, k_hi, k_lo], 1))
                        )
                    for piece in range(start, stop, LANES):
                        tau = piece // LANES
                        a = made[0][:, piece - start : piece - start + LANES]
                        b = made[1][:, piece - start : piece - start + LANES]
                        if piece == n_odd:
                            zeros.append(jnp.where(low, a, b))
                            continue
                        hi, lo = split(jnp.where(low, a, b))
                        rodd[half, 0, tau * mp : (tau + 1) * mp, to] = hi
                        rodd[half, 1, tau * mp : (tau + 1) * mp, to] = lo
                        hi, lo = split(jnp.where(low, b, a))
                        reven[half, 0, tau * mp : (tau + 1) * mp, to] = hi
                        reven[half, 1, tau * mp : (tau + 1) * mp, to] = lo
            coupled = []
            for parity, rhs in ((0, rodd), (1, reven)):
                hi, lo = rhs[half, 0], rhs[half, 1]
                coupled.append(dot_nn(c3[parity], jnp.concatenate([hi, hi, lo], 0)))
            if it == 0 and half == 0:
                for d in range(1, n_chaos):
                    gather_copy(gd, gd_send, gd_recv, d).wait()
                spread_blocks(gd)
                for p in range(pairs):
                    one, two = nat[block_at(2 * p)], nat[block_at(2 * p + 1)]
                    dg[p] = jnp.where(low, one, two) - SHIFT
            for step in range(half_pairs):
                p = half * half_pairs + step
                at = slice(step * LANES, (step + 1) * LANES)
                new = coupled[0][:, at] + swap(coupled[1][:, at]) + scale0 * zeros[step]
                new = dg[p] * vec[it, p] + new
                if it > 0:
                    new = new - GAMMA[it] * vec[it - 1, p]
                vec[it + 1, p] = new
                for j in range(it + 1):
                    add_product(j, it + 1, vec[j, p], new)
                if it < ITERS - 1:
                    add_product(it + 1, it + 1, new, new)
                    turned = swap(new)
                    ef[later][2 * p] = jnp.where(low, new, turned)
                    ef[later][2 * p + 1] = jnp.where(low, turned, new)
            if it < ITERS - 1 and half == 0:
                halo_out[it, 1] = pack(ef[later][0])
                halo_out[it, 0] = pack(ef[later][right_place])

                @pl.when(has_right)
                def _():
                    halo_copy(it, 0).start()

                @pl.when(has_left)
                def _():
                    halo_copy(it, 1).start()
        if it < ITERS - 1:
            for side in range(2):
                def read_next():
                    halo_copy(it, side).wait_recv()
                    ef[later][nbr + side] = unpack(halo_in[it, side], mp)

                fill(side, later, read_next)
            for side in range(2):
                @pl.when(has_right if side == 0 else has_left)
                def _():
                    halo_copy(it, side).wait_send()

    stat[...] = jnp.zeros_like(stat)
    for e, pair in enumerate(PAIRS):
        stat[e : e + 1, :] = jnp.sum(sums[pair], axis=0, keepdims=True)

    def reduce_copy(level, d):
        if level == 0:
            target, src, dst, send, recv = group * stage + (place + d) % stage, stat, red1.at[place], r1_send, r1_recv
        else:
            target, src, dst, send, recv = ((group + d) % n_group) * stage + place, stat, red2.at[group], r2_send, r2_recv
        return pltpu.make_async_remote_copy(
            src_ref=src, dst_ref=dst, send_sem=send.at[d], recv_sem=recv.at[d],
            device_id=(target, c), device_id_type=MESH,
        )

    red1[place] = stat[...]
    for d in range(1, stage):
        reduce_copy(0, d).start()

    mine = pl.ds(pl.multiple_of(c * hp, 8), hp)
    back = [place_of(jnp.int32(k)) for k in range(nbr)]
    for j in range(ITERS + 1):
        for p in range(pairs):
            chunk = vec[j, p, mine, :]
            turned = swap(chunk)
            natv[j, 2 * p] = jnp.where(low_hp, chunk, turned)
            natv[j, 2 * p + 1] = jnp.where(low_hp, turned, chunk)
    for j, out in enumerate((v0_out, v1_out, v2_out, v3_out)):
        for q in range(pairs):
            chunk = jnp.where(low_hp, natv[j, back[2 * q]], natv[j, back[2 * q + 1]])
            out[:, q * LANES : (q + 1) * LANES] = chunk[:modes]

    for d in range(1, stage):
        reduce_copy(0, d).wait()
    total = red1[0]
    for g in range(1, stage):
        total = total + red1[g]
    stat[...] = total
    red2[group] = total
    for d in range(1, n_group):
        reduce_copy(1, d).start()
    for d in range(1, n_group):
        reduce_copy(1, d).wait()
    total = red2[0]
    for g in range(1, n_group):
        total = total + red2[g]
    total = jnp.sum(total, axis=1, keepdims=True)
    gram = {}
    for e, (i, j) in enumerate(PAIRS):
        gram[(i, j)] = gram[(j, i)] = total[e : e + 1, :]

    def inner(one, two):
        value = None
        for i, a in one.items():
            for j, b in two.items():
                part = a * b * gram[(i, j)]
                value = part if value is None else value + part
        return value

    def plus(one, scale, two):
        result = dict(one)
        for i, a in two.items():
            result[i] = result[i] + scale * a if i in result else scale * a
        return result

    def image_of(vector):
        result = {}
        for k, a in vector.items():
            result = plus(result, a, {k: jnp.full((1, 1), SHIFT, f32), k + 1: jnp.ones((1, 1), f32)})
            if k > 0:
                result = plus(result, a, {k - 1: jnp.full((1, 1), GAMMA[k], f32)})
        return result

    residual = {0: jnp.ones((1, 1), f32)}
    direction = dict(residual)
    field = {}
    norm_now = gram[(0, 0)]
    for it in range(ITERS):
        image = image_of(direction)
        alpha = norm_now / inner(direction, image)
        field = plus(field, alpha, direction)
        residual = plus(residual, -alpha, image)
        if it < ITERS - 1:
            norm_next = inner(residual, residual)
            direction = plus(residual, norm_next / norm_now, direction)
            norm_now = norm_next

    for coefs, first in ((field, 0), (residual, 8)):
        for j, a in coefs.items():
            coef_out[first + j : first + j + 1, :] = jnp.broadcast_to(a, (1, LANES))


def per_device(right_side, diagonal, stiffness, columns, interface, triples, coupling_values):
    n_space, n_chaos = lax.axis_size("space"), lax.axis_size("chaos")
    modes, width = right_side.shape
    terms, nbr, block, depth = stiffness.shape
    hp = (modes + 7) // 8 * 8
    mp = n_chaos * hp
    pairs = nbr // 2
    even_terms = (terms - 1) // 2
    cols = even_terms * LANES + 2 * block
    stage = 1
    while stage * stage < n_space:
        stage *= 2
    n_group = n_space // stage
    f32, bf16 = jnp.float32, jnp.bfloat16
    vmem = pl.BlockSpec(memory_space=pltpu.VMEM)
    smem = pl.BlockSpec(memory_space=pltpu.SMEM)
    dma = pltpu.SemaphoreType.DMA
    out = jax.ShapeDtypeStruct((modes, width), f32)
    whole_depth = -(-even_terms * mp // 256) * 256
    *basis, coefs = pl.pallas_call(
        functools.partial(kernel, n_space, n_chaos, stage),
        out_shape=(out,) * (ITERS + 1) + (jax.ShapeDtypeStruct((16, LANES), f32),),
        in_specs=[vmem, vmem, pl.BlockSpec(memory_space=pl.ANY), smem, smem, vmem, vmem],
        out_specs=(vmem,) * (ITERS + 2),
        scratch_shapes=[
            pltpu.VMEM(stiffness.shape, f32),
            pltpu.VMEM((nbr, cols, depth), bf16),
            pltpu.VMEM((nbr, cols, depth), bf16),
            pltpu.VMEM((2, mp, 3 * whole_depth), bf16),
            pltpu.VMEM((mp, LANES), f32),
            pltpu.VMEM((n_chaos, hp, width), f32),
            pltpu.VMEM((n_chaos, hp, width), f32),
            pltpu.VMEM((nbr, mp, LANES), f32),
            pltpu.VMEM((nbr + 2, mp, LANES), f32),
            pltpu.VMEM((nbr + 2, mp, LANES), f32),
            pltpu.VMEM((ITERS + 1, pairs, mp, LANES), f32),
            pltpu.VMEM((pairs, mp, LANES), f32),
            pltpu.VMEM((nbr, mp, 2 * depth), bf16),
            pltpu.VMEM((2, 2, whole_depth, pairs // 2 * LANES), bf16),
            pltpu.VMEM((2, 2, whole_depth, pairs // 2 * LANES), bf16),
            pltpu.VMEM((2, packed_rows(hp), LANES), f32),
            pltpu.VMEM((nbr, hp, LANES), f32),
            pltpu.VMEM((2, n_chaos, packed_rows(hp), LANES), f32),
            pltpu.VMEM((ITERS - 1, 2, packed_rows(mp), LANES), f32),
            pltpu.VMEM((ITERS - 1, 2, packed_rows(mp), LANES), f32),
            pltpu.VMEM((16, LANES), f32),
            pltpu.VMEM((stage, 16, LANES), f32),
            pltpu.VMEM((n_group, 16, LANES), f32),
            pltpu.VMEM((ITERS + 1, nbr, hp, LANES), f32),
            dma,
            dma((n_chaos,)), dma((n_chaos,)), dma((n_chaos,)), dma((n_chaos,)),
            dma((2, n_chaos)), dma((2, n_chaos)),
            dma((ITERS - 1, 2)), dma((ITERS - 1, 2)),
            dma((stage,)), dma((stage,)), dma((n_group,)), dma((n_group,)),
        ],
        compiler_params=pltpu.CompilerParams(
            collective_id=0, has_side_effects=True, vmem_limit_bytes=60 * 1024 * 1024
        ),
        name="solve",
    )(
        right_side, diagonal, stiffness, columns.T, interface, triples.T,
        coupling_values,
    )
    field = sum(coefs[j, 0] * basis[j] for j in range(ITERS))
    residual = sum(coefs[8 + j, 0] * basis[j] for j in range(ITERS + 1))
    return field, residual


def solution(mesh):
    placed = (
        P("chaos", "space"),
        P("chaos", "space"),
        P(None, "space", None, None),
        P("space", None),
        P("space", None),
        P(),
        P(),
    )
    return jax.shard_map(
        per_device,
        mesh=mesh,
        in_specs=placed,
        out_specs=(P("chaos", "space"), P("chaos", "space")),
        check_vma=False,
    )
```

```python
import functools

import jax
import jax.numpy as jnp
from jax import lax
from jax.experimental import pallas as pl
from jax.experimental.pallas import tpu as pltpu
from jax.sharding import PartitionSpec as P

MESH = pl.DeviceIdType.MESH
ITERS = 3
LANES = 128
SHIFT = 2.75
GAMMA = (0.0, 0.52083333, 0.41666667)
PAIRS = ((0, 0), (0, 1), (1, 1), (0, 2), (1, 2), (2, 2), (0, 3), (1, 3), (2, 3))


def split(x):
    hi = x.astype(jnp.bfloat16)
    lo = (x - hi.astype(jnp.float32)).astype(jnp.bfloat16)
    return hi, lo


def dot_nn(a, b):
    return lax.dot_general(a, b, (((1,), (0,)), ((), ())), preferred_element_type=jnp.float32)


def low_half(shape):
    return lax.broadcasted_iota(jnp.int32, shape, len(shape) - 1) < LANES // 2


def swap(x):
    return pltpu.roll(x, LANES // 2, 1)


def packed_rows(rows):
    return (rows // 8 + 1) // 2 * 8


def pack(x):
    rows = x.shape[0]
    part = packed_rows(rows)
    return jnp.where(low_half((part, LANES)), x[:part], x[rows - part :])


def unpack(x, rows):
    part = x.shape[0]
    turned = swap(x)
    low = low_half(x.shape)
    top = jnp.where(low, x, turned)
    bottom = jnp.where(low, turned, x)
    return jnp.concatenate([top, bottom[2 * part - rows :]], 0)


def one_way(x):
    return jnp.where(x, 1, 0)


def kernel(
    n_space, n_chaos, stage,
    b_ref, d_ref, k_hbm, col_ref, if_ref, tri_ref, val_ref,
    v0_out, v1_out, v2_out, v3_out, coef_out,
    kf, khi, klo, c3, cdiag, gb, gd, nat, ef0, ef1, vec, dg, picked, rodd, reven,
    own_send, own_blocks, halo0, halo_out, halo_in, stat, red1, red2, natv,
    k_sem, gb_send, gb_recv, gd_send, gd_recv, h0_send, h0_recv, h_send, h_recv,
    r1_send, r1_recv, r2_send, r2_recv,
):
    f32 = jnp.float32
    modes, width = b_ref.shape
    hp = gb.shape[1]
    mp = n_chaos * hp
    terms, nbr, block, _ = kf.shape
    nnz = col_ref.shape[0]
    pairs = nbr // 2
    even_terms = (terms - 1) // 2
    depth = rodd.shape[2]
    ef = (ef0, ef1)
    s = lax.axis_index("space")
    c = lax.axis_index("chaos")

    k_copy = pltpu.make_async_copy(k_hbm, kf, k_sem)
    k_copy.start()

    barrier = pltpu.get_barrier_semaphore()
    group, place = s // stage, s % stage
    n_group = n_space // stage
    has_left, has_right = s > 0, s < n_space - 1

    def greet(space, chaos):
        pl.semaphore_signal(barrier, inc=1, device_id=(space, chaos), device_id_type=MESH)

    for d in range(1, n_chaos):
        greet(s, (c + d) % n_chaos)
    for d in range(n_chaos):
        @pl.when(has_left)
        def _():
            greet(s - 1, (c + d) % n_chaos)

        @pl.when(has_right)
        def _():
            greet(s + 1, (c + d) % n_chaos)
    for d in range(1, stage):
        greet(group * stage + (place + d) % stage, c)
    for d in range(1, n_group):
        greet(((group + d) % n_group) * stage + place, c)

    own_b = jnp.concatenate([b_ref[...], jnp.zeros((hp - modes, width), f32)], 0) if hp > modes else b_ref[...]
    own_d = jnp.concatenate([d_ref[...], jnp.zeros((hp - modes, width), f32)], 0) if hp > modes else d_ref[...]
    gb[c] = own_b
    gd[c] = own_d
    low_hp = low_half((hp, LANES))
    for q in range(pairs):
        chunk = own_b[:, q * LANES : (q + 1) * LANES]
        turned = swap(chunk)
        own_blocks[2 * q] = jnp.where(low_hp, chunk, turned)
        own_blocks[2 * q + 1] = jnp.where(low_hp, turned, chunk)
    if0, if1 = if_ref[0, 0], if_ref[0, 1]
    own_send[1] = pack(own_blocks[if0])
    own_send[0] = pack(own_blocks[if1])

    pl.semaphore_wait(
        barrier,
        (n_chaos - 1) + n_chaos * (one_way(has_left) + one_way(has_right)) + (stage - 1) + (n_group - 1),
    )

    def halo0_copy(side, d):
        return pltpu.make_async_remote_copy(
            src_ref=own_send.at[side], dst_ref=halo0.at[side, c],
            send_sem=h0_send.at[side, d], recv_sem=h0_recv.at[side, d],
            device_id=(s + 1 if side == 0 else s - 1, (c + d) % n_chaos), device_id_type=MESH,
        )

    def gather_copy(buf, send, recv, d):
        return pltpu.make_async_remote_copy(
            src_ref=buf.at[c], dst_ref=buf.at[c], send_sem=send.at[d], recv_sem=recv.at[d],
            device_id=(s, (c + d) % n_chaos), device_id_type=MESH,
        )

    for d in range(n_chaos):
        @pl.when(has_right)
        def _():
            halo0_copy(0, d).start()

        @pl.when(has_left)
        def _():
            halo0_copy(1, d).start()
    for d in range(1, n_chaos):
        gather_copy(gb, gb_send, gb_recv, d).start()
    for d in range(1, n_chaos):
        gather_copy(gd, gd_send, gd_recv, d).start()

    second = jnp.where(if1 == if0, jnp.where(if0 == 0, 1, 0), if1)
    small, large = jnp.minimum(if0, second), jnp.maximum(if0, second)

    def block_at(k):
        if isinstance(k, int) and k < 2:
            return if0 if k == 0 else second
        row = k - 2
        row = row + one_way(row >= small)
        return row + one_way(row >= large)

    def place_of(row):
        rest = 2 + row - one_way(if0 < row) - one_way(second < row)
        found = jnp.where(row == if0, 0, jnp.where(row == second, 1, rest))
        return jnp.where(row >= nbr, row, found)

    def slot(mode):
        shift = jnp.zeros_like(mode)
        for h in range(1, n_chaos):
            shift = shift + one_way(mode >= h * modes)
        return mode + (hp - modes) * shift

    entries = tri_ref.shape[1]
    term = tri_ref[0:1, :]
    row = slot(tri_ref[1:2, :])
    col = slot(tri_ref[2:3, :])
    values = val_ref[...].reshape(1, entries)
    hit = lax.broadcasted_iota(jnp.int32, (mp, entries), 0) == row
    spread = jnp.where(hit, values, 0.0)
    cdiag[...] = jnp.broadcast_to(
        jnp.sum(jnp.where(term == 0, spread, 0.0), axis=1, keepdims=True), (mp, LANES)
    )
    spread_hi, spread_lo = split(spread)
    spread2 = jnp.concatenate([spread_hi, spread_lo], 0)
    padded = -(-entries // LANES) * LANES
    spread2 = jnp.concatenate([spread2, jnp.zeros((2 * mp, padded - entries), spread2.dtype)], 1)
    lanes_iota = lax.broadcasted_iota(jnp.int32, (LANES, depth), 1)
    for parity in range(2):
        first = 1 if parity == 0 else 2
        mine = (term > 0) & ((term & 1) == (first & 1))
        key = jnp.where(mine, ((term - first) >> 1) * mp + col, -1)
        key = jnp.concatenate([key, jnp.full((1, padded - entries), -1, jnp.int32)], 1)
        hot = []
        for n in range(0, padded, LANES):
            down = jnp.broadcast_to(key[:, n : n + LANES], (LANES, LANES)).T
            down = jnp.concatenate([down] * (depth // LANES), 1)
            hot.append(jnp.where(lanes_iota == down, 1.0, 0.0).astype(jnp.bfloat16))
        both = dot_nn(spread2, jnp.concatenate(hot, 0)).astype(jnp.bfloat16)
        c3[parity, :, :depth] = both[:mp]
        c3[parity, :, depth : 2 * depth] = both[mp:]
        c3[parity, :, 2 * depth :] = both[:mp]
    if depth > even_terms * mp:
        rest = jnp.zeros((depth - even_terms * mp, rodd.shape[3]), jnp.bfloat16)
        for half in range(2):
            for part in range(2):
                rodd[half, part, even_terms * mp :, :] = rest
                reven[half, part, even_terms * mp :, :] = rest

    k_copy.wait()

    def prepare(j, _):
        for odd in range(2):
            k = 2 * j + odd
            source = jnp.where(k == 0, if0, jnp.where(k == 1, second, block_at(k)))
            for tau in range(even_terms + 1):
                if tau == even_terms:
                    one = two = kf[0, source]
                else:
                    one, two = kf[2 * tau + 1 + odd, source], kf[2 * tau + 2 - odd, source]
                hi, lo = split(jnp.concatenate([one, two], 0).T)
                khi[k, :, tau * LANES : (tau + 1) * LANES] = hi
                klo[k, :, tau * LANES : (tau + 1) * LANES] = lo
        return 0

    lax.fori_loop(0, pairs, prepare, 0)

    low = low_half((mp, LANES))

    def spread_blocks(buf):
        for q in range(pairs):
            for h in range(n_chaos):
                chunk = buf[h, :, q * LANES : (q + 1) * LANES]
                turned = swap(chunk)
                nat[2 * q, h * hp : (h + 1) * hp] = jnp.where(low_hp, chunk, turned)
                nat[2 * q + 1, h * hp : (h + 1) * hp] = jnp.where(low_hp, turned, chunk)

    for d in range(1, n_chaos):
        gather_copy(gb, gb_send, gb_recv, d).wait()
    spread_blocks(gb)
    for p in range(pairs):
        one, two = nat[block_at(2 * p)], nat[block_at(2 * p + 1)]
        ef0[2 * p] = one
        ef0[2 * p + 1] = two
        vec[0, p] = jnp.where(low, one, two)

    def fill(side, now, read):
        present = has_left if side == 0 else has_right

        @pl.when(present)
        def _():
            read()

        @pl.when(jnp.logical_not(present))
        def _():
            ef[now][nbr + side] = jnp.zeros((mp, LANES), f32)

    for side in range(2):
        def read_first():
            for d in range(n_chaos):
                halo0_copy(side, d).wait_recv()
            for h in range(n_chaos):
                ef0[nbr + side, h * hp : (h + 1) * hp] = unpack(halo0[side, h], hp)

        fill(side, 0, read_first)
    for side in range(2):
        @pl.when(has_right if side == 0 else has_left)
        def _():
            for d in range(n_chaos):
                halo0_copy(side, d).wait_send()

    def halo_copy(it, side):
        return pltpu.make_async_remote_copy(
            src_ref=halo_out.at[it, side], dst_ref=halo_in.at[it, side],
            send_sem=h_send.at[it, side], recv_sem=h_recv.at[it, side],
            device_id=(s + 1 if side == 0 else s - 1, c), device_id_type=MESH,
        )

    places = [[place_of(col_ref[n, block_at(k)]) for n in range(nnz)] for k in range(nbr)]
    right_place = place_of(if1)
    sums = {}

    def add_product(i, j, one, two):
        part = jnp.sum((one * two).reshape(mp // 8, 8, LANES), axis=0)
        sums[(i, j)] = sums[(i, j)] + part if (i, j) in sums else part

    for p in range(pairs):
        add_product(0, 0, vec[0, p], vec[0, p])

    scale0 = cdiag[...]
    half_pairs = pairs // 2
    n_odd = even_terms * LANES
    wide = nnz * block
    for it in range(ITERS):
        now, later = it % 2, (it + 1) % 2
        for half in range(2):
            zeros = []
            for step in range(half_pairs):
                p = half * half_pairs + step
                for k in (2 * p, 2 * p + 1):
                    at = places[k]
                    for m in range(nnz // 2):
                        hi, lo = split(jnp.where(low, ef[now][at[2 * m]], ef[now][at[2 * m + 1]]))
                        picked[k, :, m * LANES : (m + 1) * LANES] = hi
                        picked[k, :, wide + m * LANES : wide + (m + 1) * LANES] = lo
            for step in range(half_pairs):
                p = half * half_pairs + step
                to = pl.ds(step * LANES, LANES)
                for start in range(0, n_odd + 2 * block, 2 * LANES):
                    stop = min(start + 2 * LANES, n_odd + 2 * block)
                    made = []
                    for k in (2 * p, 2 * p + 1):
                        hi, lo = picked[k, :, :wide], picked[k, :, wide:]
                        k_hi, k_lo = khi[k, :, start:stop], klo[k, :, start:stop]
                        made.append(
                            dot_nn(jnp.concatenate([hi, lo, hi], 1), jnp.concatenate([k_hi, k_hi, k_lo], 0))
                        )
                    for piece in range(start, stop, LANES):
                        tau = piece // LANES
                        a = made[0][:, piece - start : piece - start + LANES]
                        b = made[1][:, piece - start : piece - start + LANES]
                        if piece == n_odd:
                            zeros.append(jnp.where(low, a, b))
                            continue
                        hi, lo = split(jnp.where(low, a, b))
                        rodd[half, 0, tau * mp : (tau + 1) * mp, to] = hi
                        rodd[half, 1, tau * mp : (tau + 1) * mp, to] = lo
                        hi, lo = split(jnp.where(low, b, a))
                        reven[half, 0, tau * mp : (tau + 1) * mp, to] = hi
                        reven[half, 1, tau * mp : (tau + 1) * mp, to] = lo
            coupled = []
            for parity, rhs in ((0, rodd), (1, reven)):
                hi, lo = rhs[half, 0], rhs[half, 1]
                coupled.append(dot_nn(c3[parity], jnp.concatenate([hi, hi, lo], 0)))
            if it == 0 and half == 0:
                for d in range(1, n_chaos):
                    gather_copy(gd, gd_send, gd_recv, d).wait()
                spread_blocks(gd)
                for p in range(pairs):
                    one, two = nat[block_at(2 * p)], nat[block_at(2 * p + 1)]
                    dg[p] = jnp.where(low, one, two) - SHIFT
            for step in range(half_pairs):
                p = half * half_pairs + step
                at = slice(step * LANES, (step + 1) * LANES)
                new = coupled[0][:, at] + swap(coupled[1][:, at]) + scale0 * zeros[step]
                new = dg[p] * vec[it, p] + new
                if it > 0:
                    new = new - GAMMA[it] * vec[it - 1, p]
                vec[it + 1, p] = new
                for j in range(it + 1):
                    add_product(j, it + 1, vec[j, p], new)
                if it < ITERS - 1:
                    add_product(it + 1, it + 1, new, new)
                    turned = swap(new)
                    ef[later][2 * p] = jnp.where(low, new, turned)
                    ef[later][2 * p + 1] = jnp.where(low, turned, new)
            if it < ITERS - 1 and half == 0:
                halo_out[it, 1] = pack(ef[later][0])
                halo_out[it, 0] = pack(ef[later][right_place])

                @pl.when(has_right)
                def _():
                    halo_copy(it, 0).start()

                @pl.when(has_left)
                def _():
                    halo_copy(it, 1).start()
        if it < ITERS - 1:
            for side in range(2):
                def read_next():
                    halo_copy(it, side).wait_recv()
                    ef[later][nbr + side] = unpack(halo_in[it, side], mp)

                fill(side, later, read_next)
            for side in range(2):
                @pl.when(has_right if side == 0 else has_left)
                def _():
                    halo_copy(it, side).wait_send()

    stat[...] = jnp.zeros_like(stat)
    for e, pair in enumerate(PAIRS):
        stat[e : e + 1, :] = jnp.sum(sums[pair], axis=0, keepdims=True)

    def reduce_copy(level, d):
        if level == 0:
            target, src, dst, send, recv = group * stage + (place + d) % stage, stat, red1.at[place], r1_send, r1_recv
        else:
            target, src, dst, send, recv = ((group + d) % n_group) * stage + place, stat, red2.at[group], r2_send, r2_recv
        return pltpu.make_async_remote_copy(
            src_ref=src, dst_ref=dst, send_sem=send.at[d], recv_sem=recv.at[d],
            device_id=(target, c), device_id_type=MESH,
        )

    red1[place] = stat[...]
    for d in range(1, stage):
        reduce_copy(0, d).start()

    mine = pl.ds(pl.multiple_of(c * hp, 8), hp)
    back = [place_of(jnp.int32(k)) for k in range(nbr)]
    for j in range(ITERS + 1):
        for p in range(pairs):
            chunk = vec[j, p, mine, :]
            turned = swap(chunk)
            natv[j, 2 * p] = jnp.where(low_hp, chunk, turned)
            natv[j, 2 * p + 1] = jnp.where(low_hp, turned, chunk)
    for j, out in enumerate((v0_out, v1_out, v2_out, v3_out)):
        for q in range(pairs):
            chunk = jnp.where(low_hp, natv[j, back[2 * q]], natv[j, back[2 * q + 1]])
            out[:, q * LANES : (q + 1) * LANES] = chunk[:modes]

    for d in range(1, stage):
        reduce_copy(0, d).wait()
    total = red1[0]
    for g in range(1, stage):
        total = total + red1[g]
    stat[...] = total
    red2[group] = total
    for d in range(1, n_group):
        reduce_copy(1, d).start()
    for d in range(1, n_group):
        reduce_copy(1, d).wait()
    total = red2[0]
    for g in range(1, n_group):
        total = total + red2[g]
    total = jnp.sum(total, axis=1, keepdims=True)
    gram = {}
    for e, (i, j) in enumerate(PAIRS):
        gram[(i, j)] = gram[(j, i)] = total[e : e + 1, :]

    def inner(one, two):
        value = None
        for i, a in one.items():
            for j, b in two.items():
                part = a * b * gram[(i, j)]
                value = part if value is None else value + part
        return value

    def plus(one, scale, two):
        result = dict(one)
        for i, a in two.items():
            result[i] = result[i] + scale * a if i in result else scale * a
        return result

    def image_of(vector):
        result = {}
        for k, a in vector.items():
            result = plus(result, a, {k: jnp.full((1, 1), SHIFT, f32), k + 1: jnp.ones((1, 1), f32)})
            if k > 0:
                result = plus(result, a, {k - 1: jnp.full((1, 1), GAMMA[k], f32)})
        return result

    residual = {0: jnp.ones((1, 1), f32)}
    direction = dict(residual)
    field = {}
    norm_now = gram[(0, 0)]
    for it in range(ITERS):
        image = image_of(direction)
        alpha = norm_now / inner(direction, image)
        field = plus(field, alpha, direction)
        residual = plus(residual, -alpha, image)
        if it < ITERS - 1:
            norm_next = inner(residual, residual)
            direction = plus(residual, norm_next / norm_now, direction)
            norm_now = norm_next

    for coefs, first in ((field, 0), (residual, 8)):
        for j, a in coefs.items():
            coef_out[first + j : first + j + 1, :] = jnp.broadcast_to(a, (1, LANES))


def combine(v0_ref, v1_ref, v2_ref, v3_ref, coef_ref, x_ref, r_ref):
    basis = (v0_ref, v1_ref, v2_ref, v3_ref)
    for q in range(0, v0_ref.shape[1], LANES):
        at = slice(q, q + LANES)
        parts = [v[:, at] for v in basis]
        x_ref[:, at] = sum(coef_ref[j : j + 1, :] * parts[j] for j in range(ITERS))
        r_ref[:, at] = sum(coef_ref[8 + j : 9 + j, :] * parts[j] for j in range(ITERS + 1))


def per_device(right_side, diagonal, stiffness, columns, interface, triples, coupling_values):
    n_space, n_chaos = lax.axis_size("space"), lax.axis_size("chaos")
    modes, width = right_side.shape
    terms, nbr, block, depth = stiffness.shape
    hp = (modes + 7) // 8 * 8
    mp = n_chaos * hp
    pairs = nbr // 2
    even_terms = (terms - 1) // 2
    cols = even_terms * LANES + 2 * block
    stage = 1
    while stage * stage < n_space:
        stage *= 2
    n_group = n_space // stage
    f32, bf16 = jnp.float32, jnp.bfloat16
    vmem = pl.BlockSpec(memory_space=pltpu.VMEM)
    smem = pl.BlockSpec(memory_space=pltpu.SMEM)
    dma = pltpu.SemaphoreType.DMA
    out = jax.ShapeDtypeStruct((modes, width), f32)
    whole_depth = -(-even_terms * mp // 256) * 256
    *basis, coefs = pl.pallas_call(
        functools.partial(kernel, n_space, n_chaos, stage),
        out_shape=(out,) * (ITERS + 1) + (jax.ShapeDtypeStruct((16, LANES), f32),),
        in_specs=[vmem, vmem, pl.BlockSpec(memory_space=pltpu.HBM), smem, smem, vmem, vmem],
        out_specs=(vmem,) * (ITERS + 2),
        scratch_shapes=[
            pltpu.VMEM(stiffness.shape, f32),
            pltpu.VMEM((nbr, depth, cols), bf16),
            pltpu.VMEM((nbr, depth, cols), bf16),
            pltpu.VMEM((2, mp, 3 * whole_depth), bf16),
            pltpu.VMEM((mp, LANES), f32),
            pltpu.VMEM((n_chaos, hp, width), f32),
            pltpu.VMEM((n_chaos, hp, width), f32),
            pltpu.VMEM((nbr, mp, LANES), f32),
            pltpu.VMEM((nbr + 2, mp, LANES), f32),
            pltpu.VMEM((nbr + 2, mp, LANES), f32),
            pltpu.VMEM((ITERS + 1, pairs, mp, LANES), f32),
            pltpu.VMEM((pairs, mp, LANES), f32),
            pltpu.VMEM((nbr, mp, 2 * depth), bf16),
            pltpu.VMEM((2, 2, whole_depth, pairs // 2 * LANES), bf16),
            pltpu.VMEM((2, 2, whole_depth, pairs // 2 * LANES), bf16),
            pltpu.VMEM((2, packed_rows(hp), LANES), f32),
            pltpu.VMEM((nbr, hp, LANES), f32),
            pltpu.VMEM((2, n_chaos, packed_rows(hp), LANES), f32),
            pltpu.VMEM((ITERS - 1, 2, packed_rows(mp), LANES), f32),
            pltpu.VMEM((ITERS - 1, 2, packed_rows(mp), LANES), f32),
            pltpu.VMEM((16, LANES), f32),
            pltpu.VMEM((stage, 16, LANES), f32),
            pltpu.VMEM((n_group, 16, LANES), f32),
            pltpu.VMEM((ITERS + 1, nbr, hp, LANES), f32),
            dma,
            dma((n_chaos,)), dma((n_chaos,)), dma((n_chaos,)), dma((n_chaos,)),
            dma((2, n_chaos)), dma((2, n_chaos)),
            dma((ITERS - 1, 2)), dma((ITERS - 1, 2)),
            dma((stage,)), dma((stage,)), dma((n_group,)), dma((n_group,)),
        ],
        compiler_params=pltpu.CompilerParams(
            collective_id=0, has_side_effects=True, vmem_limit_bytes=56 * 1024 * 1024
        ),
        name="solve",
    )(
        right_side, diagonal, stiffness, columns.T, interface, triples.T,
        coupling_values,
    )
    return pl.pallas_call(
        combine,
        out_shape=(out, out),
        in_specs=[vmem] * (ITERS + 2),
        out_specs=(vmem, vmem),
        name="combine",
    )(*basis, coefs)


def solution(mesh):
    placed = (
        P("chaos", "space"),
        P("chaos", "space"),
        P(None, "space", None, None),
        P("space", None),
        P("space", None),
        P(),
        P(),
    )
    return jax.shard_map(
        per_device,
        mesh=mesh,
        in_specs=placed,
        out_specs=(P("chaos", "space"), P("chaos", "space")),
        check_vma=False,
    )
```

```python
import functools

import jax
import jax.numpy as jnp
from jax import lax
from jax.experimental import pallas as pl
from jax.experimental.pallas import tpu as pltpu
from jax.sharding import PartitionSpec as P

MESH = pl.DeviceIdType.MESH
ITERS = 3
LANES = 128
SHIFT = 2.75
GAMMA = (0.0, 0.52083333, 0.41666667)
PAIRS = ((0, 0), (0, 1), (1, 1), (0, 2), (1, 2), (2, 2), (0, 3), (1, 3), (2, 3))


def split(x):
    hi = x.astype(jnp.bfloat16)
    lo = (x - hi.astype(jnp.float32)).astype(jnp.bfloat16)
    return hi, lo


def dot_nn(a, b):
    return lax.dot_general(a, b, (((1,), (0,)), ((), ())), preferred_element_type=jnp.float32)


def low_half(shape):
    return lax.broadcasted_iota(jnp.int32, shape, len(shape) - 1) < LANES // 2


def swap(x):
    return pltpu.roll(x, LANES // 2, 1)


def packed_rows(rows):
    return (rows // 8 + 1) // 2 * 8


def pack(x):
    rows = x.shape[0]
    part = packed_rows(rows)
    return jnp.where(low_half((part, LANES)), x[:part], x[rows - part :])


def unpack(x, rows):
    part = x.shape[0]
    turned = swap(x)
    low = low_half(x.shape)
    top = jnp.where(low, x, turned)
    bottom = jnp.where(low, turned, x)
    return jnp.concatenate([top, bottom[2 * part - rows :]], 0)


def one_way(x):
    return jnp.where(x, 1, 0)


def kernel(
    n_space, n_chaos,
    b_ref, d_ref, k_hbm, col_ref, if_ref, tri_ref, val_ref,
    v0_out, v1_out, v2_out, v3_out, coef_out,
    kf, khi, klo, c3, cdiag, gb, gd, ef0, ef1, vec, picked, rodd, reven,
    own_send, own_blocks, halo0, halo_out, halo_in, stat, red, natv,
    k_sem, gb_send, gb_recv, gd_send, gd_recv, h0_send, h0_recv, h_send, h_recv,
    r_send, r_recv,
):
    f32 = jnp.float32
    modes, width = b_ref.shape
    mp = gb.shape[1]
    hp = mp // n_chaos
    terms, nbr, block, _ = kf.shape
    nnz = col_ref.shape[0]
    pairs = nbr // 2
    even_terms = (terms - 1) // 2
    depth = rodd.shape[2]
    ef = (ef0, ef1)
    s = lax.axis_index("space")
    c = lax.axis_index("chaos")

    k_copy = pltpu.make_async_copy(k_hbm, kf, k_sem)
    k_copy.start()

    barrier = pltpu.get_barrier_semaphore()
    has_left, has_right = s > 0, s < n_space - 1

    def greet(space, chaos):
        pl.semaphore_signal(barrier, inc=1, device_id=(space, chaos), device_id_type=MESH)

    for d in range(1, n_chaos):
        greet(s, (c + d) % n_chaos)
    for d in range(n_chaos):
        @pl.when(has_left)
        def _():
            greet(s - 1, (c + d) % n_chaos)

        @pl.when(has_right)
        def _():
            greet(s + 1, (c + d) % n_chaos)
    for d in range(1, n_space):
        greet((s + d) % n_space, c)

    if0, if1 = if_ref[0, 0], if_ref[0, 1]
    second = jnp.where(if1 == if0, jnp.where(if0 == 0, 1, 0), if1)
    small, large = jnp.minimum(if0, second), jnp.maximum(if0, second)

    def block_at(k):
        if isinstance(k, int) and k < 2:
            return if0 if k == 0 else second
        row = k - 2
        row = row + one_way(row >= small)
        return row + one_way(row >= large)

    def place_of(row):
        rest = 2 + row - one_way(if0 < row) - one_way(second < row)
        found = jnp.where(row == if0, 0, jnp.where(row == second, 1, rest))
        return jnp.where(row >= nbr, row, found)

    mine = pl.ds(pl.multiple_of(c * hp, 8), hp)
    low_hp = low_half((hp, LANES))

    def own_rows(ref, which, buf):
        for q in range(pairs):
            chunk = ref[:, q * LANES : (q + 1) * LANES]
            if hp > modes:
                chunk = jnp.concatenate([chunk, jnp.zeros((hp - modes, LANES), f32)], 0)
            turned = swap(chunk)
            own_blocks[which, 2 * q] = jnp.where(low_hp, chunk, turned)
            own_blocks[which, 2 * q + 1] = jnp.where(low_hp, turned, chunk)
        for p in range(pairs):
            one, two = own_blocks[which, block_at(2 * p)], own_blocks[which, block_at(2 * p + 1)]
            buf[p, mine, :] = jnp.where(low_hp, one, two)

    own_rows(b_ref, 0, gb)
    own_send[1] = pack(own_blocks[0, if0])
    own_send[0] = pack(own_blocks[0, if1])
    own_rows(d_ref, 1, gd)

    pl.semaphore_wait(
        barrier,
        (n_chaos - 1) + n_chaos * (one_way(has_left) + one_way(has_right)) + (n_space - 1),
    )

    def halo0_copy(side, d):
        return pltpu.make_async_remote_copy(
            src_ref=own_send.at[side], dst_ref=halo0.at[side, c],
            send_sem=h0_send.at[side, d], recv_sem=h0_recv.at[side, d],
            device_id=(s + 1 if side == 0 else s - 1, (c + d) % n_chaos), device_id_type=MESH,
        )

    half_pairs = pairs // 2

    def gather_copy(buf, part, send, recv, d):
        which = buf.at[part, mine, :]
        return pltpu.make_async_remote_copy(
            src_ref=which, dst_ref=which, send_sem=send, recv_sem=recv,
            device_id=(s, (c + d) % n_chaos), device_id_type=MESH,
        )

    def b_copy(d):
        return gather_copy(gb, pl.ds(0, pairs), gb_send.at[d], gb_recv.at[d], d)

    def d_copy(half, d):
        part = pl.ds(half * half_pairs, half_pairs)
        return gather_copy(gd, part, gd_send.at[half, d], gd_recv.at[half, d], d)

    for d in range(n_chaos):
        @pl.when(has_right)
        def _():
            halo0_copy(0, d).start()

        @pl.when(has_left)
        def _():
            halo0_copy(1, d).start()
    for d in range(1, n_chaos):
        b_copy(d).start()

    def slot(mode):
        shift = jnp.zeros_like(mode)
        for h in range(1, n_chaos):
            shift = shift + one_way(mode >= h * modes)
        return mode + (hp - modes) * shift

    entries = tri_ref.shape[1]
    term = tri_ref[0:1, :]
    row = slot(tri_ref[1:2, :])
    col = slot(tri_ref[2:3, :])
    values = val_ref[...].reshape(1, entries)
    hit = lax.broadcasted_iota(jnp.int32, (mp, entries), 0) == row
    spread = jnp.where(hit, values, 0.0)
    cdiag[...] = jnp.broadcast_to(
        jnp.sum(jnp.where(term == 0, spread, 0.0), axis=1, keepdims=True), (mp, LANES)
    )
    spread_hi, spread_lo = split(spread)
    spread2 = jnp.concatenate([spread_hi, spread_lo], 0)
    padded = -(-entries // LANES) * LANES
    spread2 = jnp.concatenate([spread2, jnp.zeros((2 * mp, padded - entries), spread2.dtype)], 1)
    lanes_iota = lax.broadcasted_iota(jnp.int32, (LANES, depth), 1)
    for parity in range(2):
        first = 1 if parity == 0 else 2
        listed = (term > 0) & ((term & 1) == (first & 1))
        key = jnp.where(listed, ((term - first) >> 1) * mp + col, -1)
        key = jnp.concatenate([key, jnp.full((1, padded - entries), -1, jnp.int32)], 1)
        hot = []
        for n in range(0, padded, LANES):
            down = jnp.broadcast_to(key[:, n : n + LANES], (LANES, LANES)).T
            down = jnp.concatenate([down] * (depth // LANES), 1)
            hot.append(jnp.where(lanes_iota == down, 1.0, 0.0).astype(jnp.bfloat16))
        both = dot_nn(spread2, jnp.concatenate(hot, 0)).astype(jnp.bfloat16)
        c3[parity, :, :depth] = both[:mp]
        c3[parity, :, depth : 2 * depth] = both[mp:]
        c3[parity, :, 2 * depth :] = both[:mp]
    if depth > even_terms * mp:
        rest = jnp.zeros((depth - even_terms * mp, rodd.shape[3]), jnp.bfloat16)
        for half in range(2):
            for part in range(2):
                rodd[half, part, even_terms * mp :, :] = rest
                reven[half, part, even_terms * mp :, :] = rest

    k_copy.wait()

    def prepare(j, _):
        for odd in range(2):
            k = 2 * j + odd
            source = jnp.where(k == 0, if0, jnp.where(k == 1, second, block_at(k)))
            for tau in range(even_terms + 1):
                if tau == even_terms:
                    one = two = kf[0, source]
                else:
                    one, two = kf[2 * tau + 1 + odd, source], kf[2 * tau + 2 - odd, source]
                hi, lo = split(jnp.concatenate([one, two], 0).T)
                khi[k, :, tau * LANES : (tau + 1) * LANES] = hi
                klo[k, :, tau * LANES : (tau + 1) * LANES] = lo
        return 0

    lax.fori_loop(0, pairs, prepare, 0)

    low = low_half((mp, LANES))

    for d in range(1, n_chaos):
        b_copy(d).wait()
    for d in range(1, n_chaos):
        d_copy(0, d).start()
    for p in range(pairs):
        chunk = gb[p]
        turned = swap(chunk)
        ef0[2 * p] = jnp.where(low, chunk, turned)
        ef0[2 * p + 1] = jnp.where(low, turned, chunk)

    def fill(side, now, read):
        present = has_left if side == 0 else has_right

        @pl.when(present)
        def _():
            read()

        @pl.when(jnp.logical_not(present))
        def _():
            ef[now][nbr + side] = jnp.zeros((mp, LANES), f32)

    for side in range(2):
        def read_first():
            for d in range(n_chaos):
                halo0_copy(side, d).wait_recv()
            for h in range(n_chaos):
                ef0[nbr + side, h * hp : (h + 1) * hp] = unpack(halo0[side, h], hp)

        fill(side, 0, read_first)
    for side in range(2):
        @pl.when(has_right if side == 0 else has_left)
        def _():
            for d in range(n_chaos):
                halo0_copy(side, d).wait_send()

    def halo_copy(it, side):
        return pltpu.make_async_remote_copy(
            src_ref=halo_out.at[it, side], dst_ref=halo_in.at[it, side],
            send_sem=h_send.at[it, side], recv_sem=h_recv.at[it, side],
            device_id=(s + 1 if side == 0 else s - 1, c), device_id_type=MESH,
        )

    places = [[place_of(col_ref[n, block_at(k)]) for n in range(nnz)] for k in range(nbr)]
    right_place = place_of(if1)
    sums = {}

    def add_product(i, j, one, two):
        part = jnp.sum((one * two).reshape(mp // 8, 8, LANES), axis=0)
        sums[(i, j)] = sums[(i, j)] + part if (i, j) in sums else part

    for p in range(pairs):
        add_product(0, 0, gb[p], gb[p])

    def basis(j, p, rows=slice(None)):
        return gb[p, rows, :] if j == 0 else vec[j - 1, p, rows, :]

    scale0 = cdiag[...]
    n_odd = even_terms * LANES
    wide = nnz * block
    for it in range(ITERS):
        now, later = it % 2, (it + 1) % 2
        for half in range(2):
            zeros = []
            for step in range(half_pairs):
                p = half * half_pairs + step
                for k in (2 * p, 2 * p + 1):
                    at = places[k]
                    for m in range(nnz // 2):
                        hi, lo = split(jnp.where(low, ef[now][at[2 * m]], ef[now][at[2 * m + 1]]))
                        picked[k, :, m * LANES : (m + 1) * LANES] = hi
                        picked[k, :, wide + m * LANES : wide + (m + 1) * LANES] = lo
            for step in range(half_pairs):
                p = half * half_pairs + step
                to = pl.ds(step * LANES, LANES)
                for start in range(0, n_odd + 2 * block, 2 * LANES):
                    stop = min(start + 2 * LANES, n_odd + 2 * block)
                    made = []
                    for k in (2 * p, 2 * p + 1):
                        hi, lo = picked[k, :, :wide], picked[k, :, wide:]
                        k_hi, k_lo = khi[k, :, start:stop], klo[k, :, start:stop]
                        made.append(
                            dot_nn(jnp.concatenate([hi, lo, hi], 1), jnp.concatenate([k_hi, k_hi, k_lo], 0))
                        )
                    for piece in range(start, stop, LANES):
                        tau = piece // LANES
                        a = made[0][:, piece - start : piece - start + LANES]
                        b = made[1][:, piece - start : piece - start + LANES]
                        if piece == n_odd:
                            zeros.append(jnp.where(low, a, b))
                            continue
                        hi, lo = split(jnp.where(low, a, b))
                        rodd[half, 0, tau * mp : (tau + 1) * mp, to] = hi
                        rodd[half, 1, tau * mp : (tau + 1) * mp, to] = lo
                        hi, lo = split(jnp.where(low, b, a))
                        reven[half, 0, tau * mp : (tau + 1) * mp, to] = hi
                        reven[half, 1, tau * mp : (tau + 1) * mp, to] = lo
            coupled = []
            for parity, rhs in ((0, rodd), (1, reven)):
                hi, lo = rhs[half, 0], rhs[half, 1]
                coupled.append(dot_nn(c3[parity], jnp.concatenate([hi, hi, lo], 0)))
            if it == 0:
                for d in range(1, n_chaos):
                    d_copy(half, d).wait()
                if half == 0:
                    for d in range(1, n_chaos):
                        d_copy(1, d).start()
            for step in range(half_pairs):
                p = half * half_pairs + step
                at = slice(step * LANES, (step + 1) * LANES)
                new = coupled[0][:, at] + swap(coupled[1][:, at]) + scale0 * zeros[step]
                new = (gd[p] - SHIFT) * basis(it, p) + new
                if it > 0:
                    new = new - GAMMA[it] * basis(it - 1, p)
                vec[it, p] = new
                for j in range(it + 1):
                    add_product(j, it + 1, basis(j, p), new)
                if it < ITERS - 1:
                    add_product(it + 1, it + 1, new, new)
                    turned = swap(new)
                    ef[later][2 * p] = jnp.where(low, new, turned)
                    ef[later][2 * p + 1] = jnp.where(low, turned, new)
            if it < ITERS - 1 and half == 0:
                halo_out[it, 1] = pack(ef[later][0])
                halo_out[it, 0] = pack(ef[later][right_place])

                @pl.when(has_right)
                def _():
                    halo_copy(it, 0).start()

                @pl.when(has_left)
                def _():
                    halo_copy(it, 1).start()
        if it < ITERS - 1:
            for side in range(2):
                def read_next():
                    halo_copy(it, side).wait_recv()
                    ef[later][nbr + side] = unpack(halo_in[it, side], mp)

                fill(side, later, read_next)
            for side in range(2):
                @pl.when(has_right if side == 0 else has_left)
                def _():
                    halo_copy(it, side).wait_send()

    stat[...] = jnp.zeros_like(stat)
    for e, pair in enumerate(PAIRS):
        stat[e : e + 1, :] = jnp.sum(sums[pair], axis=0, keepdims=True)

    def reduce_copy(d):
        return pltpu.make_async_remote_copy(
            src_ref=stat, dst_ref=red.at[s], send_sem=r_send.at[d], recv_sem=r_recv.at[d],
            device_id=((s + d) % n_space, c), device_id_type=MESH,
        )

    for d in range(1, n_space):
        reduce_copy(d).start()
    red[s] = stat[...]

    back = [place_of(jnp.int32(k)) for k in range(nbr)]
    for j in range(ITERS + 1):
        for p in range(pairs):
            chunk = basis(j, p, mine)
            turned = swap(chunk)
            natv[j, 2 * p] = jnp.where(low_hp, chunk, turned)
            natv[j, 2 * p + 1] = jnp.where(low_hp, turned, chunk)
    for j, out in enumerate((v0_out, v1_out, v2_out, v3_out)):
        for q in range(pairs):
            chunk = jnp.where(low_hp, natv[j, back[2 * q]], natv[j, back[2 * q + 1]])
            out[:, q * LANES : (q + 1) * LANES] = chunk[:modes]

    for d in range(1, n_space):
        reduce_copy(d).wait()
    total = red[0]
    for g in range(1, n_space):
        total = total + red[g]
    total = jnp.sum(total, axis=1, keepdims=True)
    gram = {}
    for e, (i, j) in enumerate(PAIRS):
        gram[(i, j)] = gram[(j, i)] = total[e : e + 1, :]

    def inner(one, two):
        value = None
        for i, a in one.items():
            for j, b in two.items():
                part = a * b * gram[(i, j)]
                value = part if value is None else value + part
        return value

    def plus(one, scale, two):
        result = dict(one)
        for i, a in two.items():
            result[i] = result[i] + scale * a if i in result else scale * a
        return result

    def image_of(vector):
        result = {}
        for k, a in vector.items():
            result = plus(result, a, {k: jnp.full((1, 1), SHIFT, f32), k + 1: jnp.ones((1, 1), f32)})
            if k > 0:
                result = plus(result, a, {k - 1: jnp.full((1, 1), GAMMA[k], f32)})
        return result

    residual = {0: jnp.ones((1, 1), f32)}
    direction = dict(residual)
    field = {}
    norm_now = gram[(0, 0)]
    for it in range(ITERS):
        image = image_of(direction)
        alpha = norm_now / inner(direction, image)
        field = plus(field, alpha, direction)
        residual = plus(residual, -alpha, image)
        if it < ITERS - 1:
            norm_next = inner(residual, residual)
            direction = plus(residual, norm_next / norm_now, direction)
            norm_now = norm_next

    for coefs, first in ((field, 0), (residual, 8)):
        for j, a in coefs.items():
            coef_out[first + j : first + j + 1, :] = jnp.broadcast_to(a, (1, LANES))


def combine(v0_ref, v1_ref, v2_ref, v3_ref, coef_ref, x_ref, r_ref):
    basis = (v0_ref, v1_ref, v2_ref, v3_ref)
    for q in range(0, v0_ref.shape[1], LANES):
        at = slice(q, q + LANES)
        parts = [v[:, at] for v in basis]
        x_ref[:, at] = sum(coef_ref[j : j + 1, :] * parts[j] for j in range(ITERS))
        r_ref[:, at] = sum(coef_ref[8 + j : 9 + j, :] * parts[j] for j in range(ITERS + 1))


def per_device(right_side, diagonal, stiffness, columns, interface, triples, coupling_values):
    n_space, n_chaos = lax.axis_size("space"), lax.axis_size("chaos")
    modes, width = right_side.shape
    terms, nbr, block, depth = stiffness.shape
    hp = (modes + 7) // 8 * 8
    mp = n_chaos * hp
    pairs = nbr // 2
    even_terms = (terms - 1) // 2
    cols = even_terms * LANES + 2 * block
    f32, bf16 = jnp.float32, jnp.bfloat16
    vmem = pl.BlockSpec(memory_space=pltpu.VMEM)
    smem = pl.BlockSpec(memory_space=pltpu.SMEM)
    dma = pltpu.SemaphoreType.DMA
    out = jax.ShapeDtypeStruct((modes, width), f32)
    whole_depth = -(-even_terms * mp // 256) * 256
    *basis, coefs = pl.pallas_call(
        functools.partial(kernel, n_space, n_chaos),
        out_shape=(out,) * (ITERS + 1) + (jax.ShapeDtypeStruct((16, LANES), f32),),
        in_specs=[vmem, vmem, pl.BlockSpec(memory_space=pltpu.HBM), smem, smem, vmem, vmem],
        out_specs=(vmem,) * (ITERS + 2),
        scratch_shapes=[
            pltpu.VMEM(stiffness.shape, f32),
            pltpu.VMEM((nbr, depth, cols), bf16),
            pltpu.VMEM((nbr, depth, cols), bf16),
            pltpu.VMEM((2, mp, 3 * whole_depth), bf16),
            pltpu.VMEM((mp, LANES), f32),
            pltpu.VMEM((pairs, mp, LANES), f32),
            pltpu.VMEM((pairs, mp, LANES), f32),
            pltpu.VMEM((nbr + 2, mp, LANES), f32),
            pltpu.VMEM((nbr + 2, mp, LANES), f32),
            pltpu.VMEM((ITERS, pairs, mp, LANES), f32),
            pltpu.VMEM((nbr, mp, 2 * depth), bf16),
            pltpu.VMEM((2, 2, whole_depth, pairs // 2 * LANES), bf16),
            pltpu.VMEM((2, 2, whole_depth, pairs // 2 * LANES), bf16),
            pltpu.VMEM((2, packed_rows(hp), LANES), f32),
            pltpu.VMEM((2, nbr, hp, LANES), f32),
            pltpu.VMEM((2, n_chaos, packed_rows(hp), LANES), f32),
            pltpu.VMEM((ITERS - 1, 2, packed_rows(mp), LANES), f32),
            pltpu.VMEM((ITERS - 1, 2, packed_rows(mp), LANES), f32),
            pltpu.VMEM((16, LANES), f32),
            pltpu.VMEM((n_space, 16, LANES), f32),
            pltpu.VMEM((ITERS + 1, nbr, hp, LANES), f32),
            dma,
            dma((n_chaos,)), dma((n_chaos,)), dma((2, n_chaos)), dma((2, n_chaos)),
            dma((2, n_chaos)), dma((2, n_chaos)),
            dma((ITERS - 1, 2)), dma((ITERS - 1, 2)),
            dma((n_space,)), dma((n_space,)),
        ],
        compiler_params=pltpu.CompilerParams(
            collective_id=0, has_side_effects=True, vmem_limit_bytes=56 * 1024 * 1024
        ),
        name="solve",
    )(
        right_side, diagonal, stiffness, columns.T, interface, triples.T,
        coupling_values,
    )
    return pl.pallas_call(
        combine,
        out_shape=(out, out),
        in_specs=[vmem] * (ITERS + 2),
        out_specs=(vmem, vmem),
        name="combine",
    )(*basis, coefs)


def solution(mesh):
    placed = (
        P("chaos", "space"),
        P("chaos", "space"),
        P(None, "space", None, None),
        P("space", None),
        P("space", None),
        P(),
        P(),
    )
    return jax.shard_map(
        per_device,
        mesh=mesh,
        in_specs=placed,
        out_specs=(P("chaos", "space"), P("chaos", "space")),
        check_vma=False,
    )
```

```python
import functools

import jax
import jax.numpy as jnp
from jax import lax
from jax.experimental import pallas as pl
from jax.experimental.pallas import tpu as pltpu
from jax.sharding import PartitionSpec as P

MESH = pl.DeviceIdType.MESH
ITERS = 3
LANES = 128
SHIFT = 2.75
GAMMA = (0.0, 0.52083333, 0.41666667)
PAIRS = ((0, 0), (0, 1), (1, 1), (0, 2), (1, 2), (2, 2), (0, 3), (1, 3), (2, 3))


def split(x):
    hi = x.astype(jnp.bfloat16)
    lo = (x - hi.astype(jnp.float32)).astype(jnp.bfloat16)
    return hi, lo


def dot_nn(a, b):
    return lax.dot_general(a, b, (((1,), (0,)), ((), ())), preferred_element_type=jnp.float32)


def low_half(shape):
    return lax.broadcasted_iota(jnp.int32, shape, len(shape) - 1) < LANES // 2


def swap(x):
    return pltpu.roll(x, LANES // 2, 1)


def packed_rows(rows):
    return (rows // 8 + 1) // 2 * 8


def pack(x):
    rows = x.shape[0]
    part = packed_rows(rows)
    return jnp.where(low_half((part, LANES)), x[:part], x[rows - part :])


def unpack(x, rows):
    part = x.shape[0]
    turned = swap(x)
    low = low_half(x.shape)
    top = jnp.where(low, x, turned)
    bottom = jnp.where(low, turned, x)
    return jnp.concatenate([top, bottom[2 * part - rows :]], 0)


def one_way(x):
    return jnp.where(x, 1, 0)


def kernel(
    n_space, n_chaos,
    b_ref, d_ref, k_hbm, col_ref, if_ref, tri_ref, val_ref,
    basis_out, coef_out,
    kf, khi, klo, c3, cdiag, gb, gd, ef, vec, picked, rodd, reven,
    own_send, own_blocks, halo0, halo_out, halo_in, stat, red, natv,
    k_sem, gb_send, gb_recv, gd_send, gd_recv, h0_send, h0_recv, h_send, h_recv,
    r_send, r_recv,
):
    f32 = jnp.float32
    modes, width = b_ref.shape
    mp = gb.shape[1]
    hp = mp // n_chaos
    terms, nbr, block, _ = kf.shape
    nnz = col_ref.shape[0]
    pairs = nbr // 2
    even_terms = (terms - 1) // 2
    depth = rodd.shape[1]
    s = lax.axis_index("space")
    c = lax.axis_index("chaos")

    k_copy = pltpu.make_async_copy(k_hbm, kf, k_sem)
    k_copy.start()

    barrier = pltpu.get_barrier_semaphore()
    has_left, has_right = s > 0, s < n_space - 1

    def greet(space, chaos):
        pl.semaphore_signal(barrier, inc=1, device_id=(space, chaos), device_id_type=MESH)

    for d in range(1, n_chaos):
        greet(s, (c + d) % n_chaos)
    for d in range(n_chaos):
        @pl.when(has_left)
        def _():
            greet(s - 1, (c + d) % n_chaos)

        @pl.when(has_right)
        def _():
            greet(s + 1, (c + d) % n_chaos)
    for d in range(1, n_space):
        greet((s + d) % n_space, c)

    if0, if1 = if_ref[0, 0], if_ref[0, 1]
    second = jnp.where(if1 == if0, jnp.where(if0 == 0, 1, 0), if1)
    small, large = jnp.minimum(if0, second), jnp.maximum(if0, second)

    def block_at(k):
        if isinstance(k, int) and k < 2:
            return if0 if k == 0 else second
        row = k - 2
        row = row + one_way(row >= small)
        row = row + one_way(row >= large)
        return row if isinstance(k, int) else jnp.where(k == 0, if0, jnp.where(k == 1, second, row))

    def place_of(row):
        rest = 2 + row - one_way(if0 < row) - one_way(second < row)
        found = jnp.where(row == if0, 0, jnp.where(row == second, 1, rest))
        return jnp.where(row >= nbr, row, found)

    mine = pl.ds(pl.multiple_of(c * hp, 8), hp)
    low_hp = low_half((hp, LANES))

    def own_rows(ref, which, buf):
        for q in range(pairs):
            chunk = ref[:, q * LANES : (q + 1) * LANES]
            if hp > modes:
                chunk = jnp.concatenate([chunk, jnp.zeros((hp - modes, LANES), f32)], 0)
            turned = swap(chunk)
            own_blocks[which, 2 * q] = jnp.where(low_hp, chunk, turned)
            own_blocks[which, 2 * q + 1] = jnp.where(low_hp, turned, chunk)
        for p in range(pairs):
            one, two = own_blocks[which, block_at(2 * p)], own_blocks[which, block_at(2 * p + 1)]
            buf[p, mine, :] = jnp.where(low_hp, one, two)

    own_rows(b_ref, 0, gb)
    own_send[1] = pack(own_blocks[0, if0])
    own_send[0] = pack(own_blocks[0, if1])
    own_rows(d_ref, 1, gd)

    pl.semaphore_wait(
        barrier,
        (n_chaos - 1) + n_chaos * (one_way(has_left) + one_way(has_right)) + (n_space - 1),
    )

    def halo0_copy(side, d):
        return pltpu.make_async_remote_copy(
            src_ref=own_send.at[side], dst_ref=halo0.at[side, c],
            send_sem=h0_send.at[side, d], recv_sem=h0_recv.at[side, d],
            device_id=(s + 1 if side == 0 else s - 1, (c + d) % n_chaos), device_id_type=MESH,
        )

    half_pairs = pairs // 2

    def gather_copy(buf, part, send, recv, d):
        which = buf.at[part, mine, :]
        return pltpu.make_async_remote_copy(
            src_ref=which, dst_ref=which, send_sem=send, recv_sem=recv,
            device_id=(s, (c + d) % n_chaos), device_id_type=MESH,
        )

    def b_copy(d):
        return gather_copy(gb, pl.ds(0, pairs), gb_send.at[d], gb_recv.at[d], d)

    def d_copy(half, d):
        part = pl.ds(half * half_pairs, half_pairs)
        return gather_copy(gd, part, gd_send.at[half, d], gd_recv.at[half, d], d)

    for d in range(n_chaos):
        @pl.when(has_right)
        def _():
            halo0_copy(0, d).start()

        @pl.when(has_left)
        def _():
            halo0_copy(1, d).start()
    for d in range(1, n_chaos):
        b_copy(d).start()

    def slot(mode):
        shift = jnp.zeros_like(mode)
        for h in range(1, n_chaos):
            shift = shift + one_way(mode >= h * modes)
        return mode + (hp - modes) * shift

    entries = tri_ref.shape[1]
    term = tri_ref[0:1, :]
    row = slot(tri_ref[1:2, :])
    col = slot(tri_ref[2:3, :])
    values = val_ref[...].reshape(1, entries)
    hit = lax.broadcasted_iota(jnp.int32, (mp, entries), 0) == row
    spread = jnp.where(hit, values, 0.0)
    cdiag[...] = jnp.broadcast_to(
        jnp.sum(jnp.where(term == 0, spread, 0.0), axis=1, keepdims=True), (mp, LANES)
    )
    spread_hi, spread_lo = split(spread)
    spread2 = jnp.concatenate([spread_hi, spread_lo], 0)
    padded = -(-entries // LANES) * LANES
    spread2 = jnp.concatenate([spread2, jnp.zeros((2 * mp, padded - entries), spread2.dtype)], 1)
    lanes_iota = lax.broadcasted_iota(jnp.int32, (LANES, depth), 1)

    def table(parity, _):
        first = 1 + parity
        listed = (term > 0) & ((term & 1) == 1 - parity)
        key = jnp.where(listed, ((term - first) >> 1) * mp + col, -1)
        key = jnp.concatenate([key, jnp.full((1, padded - entries), -1, jnp.int32)], 1)
        hot = []
        for n in range(0, padded, LANES):
            down = jnp.broadcast_to(key[:, n : n + LANES], (LANES, LANES)).T
            down = jnp.concatenate([down] * (depth // LANES), 1)
            hot.append(jnp.where(lanes_iota == down, 1.0, 0.0).astype(jnp.bfloat16))
        both = dot_nn(spread2, jnp.concatenate(hot, 0)).astype(jnp.bfloat16)
        c3[parity, :, :depth] = both[:mp]
        c3[parity, :, depth : 2 * depth] = both[mp:]
        c3[parity, :, 2 * depth :] = both[:mp]
        return 0

    lax.fori_loop(0, 2, table, 0)
    if depth > even_terms * mp:
        rest = jnp.zeros((depth - even_terms * mp, rodd.shape[2]), jnp.bfloat16)
        for part in range(2):
            rodd[part, even_terms * mp :, :] = rest
            reven[part, even_terms * mp :, :] = rest

    k_copy.wait()

    def prepare(j, _):
        for odd in range(2):
            k = 2 * j + odd
            source = block_at(k)
            for tau in range(even_terms + 1):
                if tau == even_terms:
                    one = two = kf[0, source]
                else:
                    one, two = kf[2 * tau + 1 + odd, source], kf[2 * tau + 2 - odd, source]
                hi, lo = split(jnp.concatenate([one, two], 0).T)
                khi[k, :, tau * LANES : (tau + 1) * LANES] = hi
                klo[k, :, tau * LANES : (tau + 1) * LANES] = lo
        return 0

    lax.fori_loop(0, pairs, prepare, 0)

    low = low_half((mp, LANES))

    for d in range(1, n_chaos):
        b_copy(d).wait()
    for d in range(1, n_chaos):
        d_copy(0, d).start()
    for p in range(pairs):
        chunk = gb[p]
        turned = swap(chunk)
        vec[0, p] = chunk
        ef[0, 2 * p] = jnp.where(low, chunk, turned)
        ef[0, 2 * p + 1] = jnp.where(low, turned, chunk)

    def fill(side, now, read):
        present = has_left if side == 0 else has_right

        @pl.when(present)
        def _():
            read()

        @pl.when(jnp.logical_not(present))
        def _():
            ef[now, nbr + side] = jnp.zeros((mp, LANES), f32)

    for side in range(2):
        def read_first():
            for d in range(n_chaos):
                halo0_copy(side, d).wait_recv()
            for h in range(n_chaos):
                ef[0, nbr + side, h * hp : (h + 1) * hp] = unpack(halo0[side, h], hp)

        fill(side, 0, read_first)
    for side in range(2):
        @pl.when(has_right if side == 0 else has_left)
        def _():
            for d in range(n_chaos):
                halo0_copy(side, d).wait_send()

    def halo_copy(it, side):
        return pltpu.make_async_remote_copy(
            src_ref=halo_out.at[it, side], dst_ref=halo_in.at[it, side],
            send_sem=h_send.at[it, side], recv_sem=h_recv.at[it, side],
            device_id=(s + 1 if side == 0 else s - 1, c), device_id_type=MESH,
        )

    right_place = place_of(if1)
    scale0 = cdiag[...]
    n_odd = even_terms * LANES
    wide = nnz * block
    per_half = 2 * half_pairs

    def half_step(it, half):
        now = it % 2
        later = 1 - now
        for i in range(per_half):
            row = block_at(half * per_half + i)
            at = [place_of(col_ref[n, row]) for n in range(nnz)]
            for m in range(nnz // 2):
                hi, lo = split(jnp.where(low, ef[now, at[2 * m]], ef[now, at[2 * m + 1]]))
                picked[i, :, m * LANES : (m + 1) * LANES] = hi
                picked[i, :, wide + m * LANES : wide + (m + 1) * LANES] = lo
        zeros = []
        for step in range(half_pairs):
            to = pl.ds(step * LANES, LANES)
            for start in range(0, n_odd + 2 * block, 2 * LANES):
                stop = min(start + 2 * LANES, n_odd + 2 * block)
                made = []
                for i in (2 * step, 2 * step + 1):
                    k = half * per_half + i
                    hi, lo = picked[i, :, :wide], picked[i, :, wide:]
                    k_hi, k_lo = khi[k, :, start:stop], klo[k, :, start:stop]
                    made.append(
                        dot_nn(jnp.concatenate([hi, lo, hi], 1), jnp.concatenate([k_hi, k_hi, k_lo], 0))
                    )
                for piece in range(start, stop, LANES):
                    tau = piece // LANES
                    a = made[0][:, piece - start : piece - start + LANES]
                    b = made[1][:, piece - start : piece - start + LANES]
                    if piece == n_odd:
                        zeros.append(jnp.where(low, a, b))
                        continue
                    hi, lo = split(jnp.where(low, a, b))
                    rodd[0, tau * mp : (tau + 1) * mp, to] = hi
                    rodd[1, tau * mp : (tau + 1) * mp, to] = lo
                    hi, lo = split(jnp.where(low, b, a))
                    reven[0, tau * mp : (tau + 1) * mp, to] = hi
                    reven[1, tau * mp : (tau + 1) * mp, to] = lo
        coupled = []
        for parity, rhs in ((0, rodd), (1, reven)):
            hi, lo = rhs[0], rhs[1]
            coupled.append(dot_nn(c3[parity], jnp.concatenate([hi, hi, lo], 0)))

        @pl.when(it == 0)
        def _():
            for d in range(1, n_chaos):
                d_copy(half, d).wait()

            @pl.when(half == 0)
            def _():
                for d in range(1, n_chaos):
                    d_copy(1, d).start()

        gamma = jnp.where(it == 1, GAMMA[1], jnp.where(it == 2, GAMMA[2], GAMMA[0])).astype(f32)
        for step in range(half_pairs):
            p = half * half_pairs + step
            at = slice(step * LANES, (step + 1) * LANES)
            new = coupled[0][:, at] + swap(coupled[1][:, at]) + scale0 * zeros[step]
            new = (gd[p] - SHIFT) * vec[it, p] + new - gamma * vec[jnp.maximum(it - 1, 0), p]
            vec[it + 1, p] = new
            turned = swap(new)
            ef[later, 2 * p] = jnp.where(low, new, turned)
            ef[later, 2 * p + 1] = jnp.where(low, turned, new)

        @pl.when((half == 0) & (it < ITERS - 1))
        def _():
            halo_out[it, 1] = pack(ef[later, 0])
            halo_out[it, 0] = pack(ef[later, right_place])

            @pl.when(has_right)
            def _():
                halo_copy(it, 0).start()

            @pl.when(has_left)
            def _():
                halo_copy(it, 1).start()

    def iteration(it, _):
        def one_half(half, _):
            half_step(it, half)
            return 0

        lax.fori_loop(0, 2, one_half, 0)

        @pl.when(it < ITERS - 1)
        def _():
            later = 1 - it % 2
            for side in range(2):
                def read_next():
                    halo_copy(it, side).wait_recv()
                    ef[later, nbr + side] = unpack(halo_in[it, side], mp)

                fill(side, later, read_next)
            for side in range(2):
                @pl.when(has_right if side == 0 else has_left)
                def _():
                    halo_copy(it, side).wait_send()

        return 0

    lax.fori_loop(0, ITERS, iteration, 0)

    def products(p, sums):
        parts = [vec[j, p] for j in range(ITERS + 1)]
        return tuple(
            total + jnp.sum((parts[i] * parts[j]).reshape(mp // 8, 8, LANES), axis=0)
            for total, (i, j) in zip(sums, PAIRS)
        )

    sums = lax.fori_loop(0, pairs, products, tuple(jnp.zeros((8, LANES), f32) for _ in PAIRS))

    stat[...] = jnp.zeros_like(stat)
    for e, part in enumerate(sums):
        stat[e : e + 1, :] = jnp.sum(part, axis=0, keepdims=True)

    def reduce_copy(d):
        return pltpu.make_async_remote_copy(
            src_ref=stat, dst_ref=red.at[s], send_sem=r_send.at[d], recv_sem=r_recv.at[d],
            device_id=((s + d) % n_space, c), device_id_type=MESH,
        )

    for d in range(1, n_space):
        reduce_copy(d).start()
    red[s] = stat[...]

    back = [place_of(jnp.int32(k)) for k in range(nbr)]

    def restore(j, _):
        for p in range(pairs):
            chunk = vec[j, p, mine, :]
            turned = swap(chunk)
            natv[2 * p] = jnp.where(low_hp, chunk, turned)
            natv[2 * p + 1] = jnp.where(low_hp, turned, chunk)
        for q in range(pairs):
            chunk = jnp.where(low_hp, natv[back[2 * q]], natv[back[2 * q + 1]])
            basis_out[j, :, q * LANES : (q + 1) * LANES] = chunk[:modes]
        return 0

    lax.fori_loop(0, ITERS + 1, restore, 0)

    for d in range(1, n_space):
        reduce_copy(d).wait()
    total = red[0]
    for g in range(1, n_space):
        total = total + red[g]
    total = jnp.sum(total, axis=1, keepdims=True)
    gram = {}
    for e, (i, j) in enumerate(PAIRS):
        gram[(i, j)] = gram[(j, i)] = total[e : e + 1, :]

    def inner(one, two):
        value = None
        for i, a in one.items():
            for j, b in two.items():
                part = a * b * gram[(i, j)]
                value = part if value is None else value + part
        return value

    def plus(one, scale, two):
        result = dict(one)
        for i, a in two.items():
            result[i] = result[i] + scale * a if i in result else scale * a
        return result

    def image_of(vector):
        result = {}
        for k, a in vector.items():
            result = plus(result, a, {k: jnp.full((1, 1), SHIFT, f32), k + 1: jnp.ones((1, 1), f32)})
            if k > 0:
                result = plus(result, a, {k - 1: jnp.full((1, 1), GAMMA[k], f32)})
        return result

    residual = {0: jnp.ones((1, 1), f32)}
    direction = dict(residual)
    field = {}
    norm_now = gram[(0, 0)]
    for it in range(ITERS):
        image = image_of(direction)
        alpha = norm_now / inner(direction, image)
        field = plus(field, alpha, direction)
        residual = plus(residual, -alpha, image)
        if it < ITERS - 1:
            norm_next = inner(residual, residual)
            direction = plus(residual, norm_next / norm_now, direction)
            norm_now = norm_next

    for coefs, first in ((field, 0), (residual, 8)):
        for j, a in coefs.items():
            coef_out[first + j : first + j + 1, :] = jnp.broadcast_to(a, (1, LANES))


def combine(basis_ref, coef_ref, x_ref, r_ref):
    for q in range(0, x_ref.shape[1], LANES):
        at = slice(q, q + LANES)
        parts = [basis_ref[j, :, at] for j in range(ITERS + 1)]
        x_ref[:, at] = sum(coef_ref[j : j + 1, :] * parts[j] for j in range(ITERS))
        r_ref[:, at] = sum(coef_ref[8 + j : 9 + j, :] * parts[j] for j in range(ITERS + 1))


def per_device(right_side, diagonal, stiffness, columns, interface, triples, coupling_values):
    n_space, n_chaos = lax.axis_size("space"), lax.axis_size("chaos")
    modes, width = right_side.shape
    terms, nbr, block, depth = stiffness.shape
    hp = (modes + 7) // 8 * 8
    mp = n_chaos * hp
    pairs = nbr // 2
    even_terms = (terms - 1) // 2
    cols = even_terms * LANES + 2 * block
    f32, bf16 = jnp.float32, jnp.bfloat16
    vmem = pl.BlockSpec(memory_space=pltpu.VMEM)
    smem = pl.BlockSpec(memory_space=pltpu.SMEM)
    dma = pltpu.SemaphoreType.DMA
    out = jax.ShapeDtypeStruct((modes, width), f32)
    whole_depth = -(-even_terms * mp // 256) * 256
    basis, coefs = pl.pallas_call(
        functools.partial(kernel, n_space, n_chaos),
        out_shape=(
            jax.ShapeDtypeStruct((ITERS + 1, modes, width), f32),
            jax.ShapeDtypeStruct((16, LANES), f32),
        ),
        in_specs=[vmem, vmem, pl.BlockSpec(memory_space=pltpu.HBM), smem, smem, vmem, vmem],
        out_specs=(vmem, vmem),
        scratch_shapes=[
            pltpu.VMEM(stiffness.shape, f32),
            pltpu.VMEM((nbr, depth, cols), bf16),
            pltpu.VMEM((nbr, depth, cols), bf16),
            pltpu.VMEM((2, mp, 3 * whole_depth), bf16),
            pltpu.VMEM((mp, LANES), f32),
            pltpu.VMEM((pairs, mp, LANES), f32),
            pltpu.VMEM((pairs, mp, LANES), f32),
            pltpu.VMEM((2, nbr + 2, mp, LANES), f32),
            pltpu.VMEM((ITERS + 1, pairs, mp, LANES), f32),
            pltpu.VMEM((nbr // 2, mp, 2 * depth), bf16),
            pltpu.VMEM((2, whole_depth, pairs // 2 * LANES), bf16),
            pltpu.VMEM((2, whole_depth, pairs // 2 * LANES), bf16),
            pltpu.VMEM((2, packed_rows(hp), LANES), f32),
            pltpu.VMEM((2, nbr, hp, LANES), f32),
            pltpu.VMEM((2, n_chaos, packed_rows(hp), LANES), f32),
            pltpu.VMEM((ITERS - 1, 2, packed_rows(mp), LANES), f32),
            pltpu.VMEM((ITERS - 1, 2, packed_rows(mp), LANES), f32),
            pltpu.VMEM((16, LANES), f32),
            pltpu.VMEM((n_space, 16, LANES), f32),
            pltpu.VMEM((nbr, hp, LANES), f32),
            dma,
            dma((n_chaos,)), dma((n_chaos,)), dma((2, n_chaos)), dma((2, n_chaos)),
            dma((2, n_chaos)), dma((2, n_chaos)),
            dma((ITERS - 1, 2)), dma((ITERS - 1, 2)),
            dma((n_space,)), dma((n_space,)),
        ],
        compiler_params=pltpu.CompilerParams(
            collective_id=0, has_side_effects=True, vmem_limit_bytes=56 * 1024 * 1024
        ),
        name="solve",
    )(
        right_side, diagonal, stiffness, columns.T, interface, triples.T,
        coupling_values,
    )
    return pl.pallas_call(
        combine,
        out_shape=(out, out),
        in_specs=[vmem, vmem],
        out_specs=(vmem, vmem),
        name="combine",
    )(basis, coefs)


def solution(mesh):
    placed = (
        P("chaos", "space"),
        P("chaos", "space"),
        P(None, "space", None, None),
        P("space", None),
        P("space", None),
        P(),
        P(),
    )
    return jax.shard_map(
        per_device,
        mesh=mesh,
        in_specs=placed,
        out_specs=(P("chaos", "space"), P("chaos", "space")),
        check_vma=False,
    )
```

```python
import functools

import jax
import jax.numpy as jnp
from jax import lax
from jax.experimental import pallas as pl
from jax.experimental.pallas import tpu as pltpu
from jax.sharding import PartitionSpec as P

MESH = pl.DeviceIdType.MESH
ITERS = 3
LANES = 128
SHIFT = 2.75
GAMMA = (0.0, 0.52083333, 0.41666667)
PAIRS = ((0, 0), (0, 1), (1, 1), (0, 2), (1, 2), (2, 2), (0, 3), (1, 3), (2, 3))


def split(x):
    hi = x.astype(jnp.bfloat16)
    lo = (x - hi.astype(jnp.float32)).astype(jnp.bfloat16)
    return hi, lo


def dot_nn(a, b):
    return lax.dot_general(a, b, (((1,), (0,)), ((), ())), preferred_element_type=jnp.float32)


def low_half(shape):
    return lax.broadcasted_iota(jnp.int32, shape, len(shape) - 1) < LANES // 2


def swap(x):
    return pltpu.roll(x, LANES // 2, 1)


def packed_rows(rows):
    return (rows // 8 + 1) // 2 * 8


def pack(x):
    rows = x.shape[0]
    part = packed_rows(rows)
    return jnp.where(low_half((part, LANES)), x[:part], x[rows - part :])


def unpack(x, rows):
    part = x.shape[0]
    turned = swap(x)
    low = low_half(x.shape)
    top = jnp.where(low, x, turned)
    bottom = jnp.where(low, turned, x)
    return jnp.concatenate([top, bottom[2 * part - rows :]], 0)


def one_way(x):
    return jnp.where(x, 1, 0)


def kernel(
    n_space, n_chaos,
    b_ref, d_ref, k_hbm, col_ref, if_ref, tri_ref, val_ref,
    basis_out, coef_out,
    kf, khi, klo, c3, cdiag, gb, gd, ef, vec, picked, rodd, reven,
    own_send, own_blocks, halo0, halo_out, halo_in, stat, red, natv,
    k_sem, gb_send, gb_recv, gd_send, gd_recv, h0_send, h0_recv, h_send, h_recv,
    r_send, r_recv,
):
    f32 = jnp.float32
    modes, width = b_ref.shape
    mp = gb.shape[1]
    hp = mp // n_chaos
    terms, nbr, block, _ = kf.shape
    nnz = col_ref.shape[0]
    pairs = nbr // 2
    even_terms = (terms - 1) // 2
    depth = rodd.shape[1]
    s = lax.axis_index("space")
    c = lax.axis_index("chaos")

    k_copy = pltpu.make_async_copy(k_hbm, kf, k_sem)
    k_copy.start()

    barrier = pltpu.get_barrier_semaphore()
    has_left, has_right = s > 0, s < n_space - 1

    def greet(space, chaos):
        pl.semaphore_signal(barrier, inc=1, device_id=(space, chaos), device_id_type=MESH)

    for d in range(1, n_chaos):
        greet(s, (c + d) % n_chaos)
    for d in range(n_chaos):
        @pl.when(has_left)
        def _():
            greet(s - 1, (c + d) % n_chaos)

        @pl.when(has_right)
        def _():
            greet(s + 1, (c + d) % n_chaos)
    for d in range(1, n_space):
        greet((s + d) % n_space, c)

    if0, if1 = if_ref[0, 0], if_ref[0, 1]
    second = jnp.where(if1 == if0, jnp.where(if0 == 0, 1, 0), if1)
    small, large = jnp.minimum(if0, second), jnp.maximum(if0, second)

    def block_at(k):
        if isinstance(k, int) and k < 2:
            return if0 if k == 0 else second
        row = k - 2
        row = row + one_way(row >= small)
        row = row + one_way(row >= large)
        return row if isinstance(k, int) else jnp.where(k == 0, if0, jnp.where(k == 1, second, row))

    def place_of(row):
        rest = 2 + row - one_way(if0 < row) - one_way(second < row)
        found = jnp.where(row == if0, 0, jnp.where(row == second, 1, rest))
        return jnp.where(row >= nbr, row, found)

    mine = pl.ds(pl.multiple_of(c * hp, 8), hp)
    low_hp = low_half((hp, LANES))

    def own_rows(ref, which, buf):
        for q in range(pairs):
            chunk = ref[:, q * LANES : (q + 1) * LANES]
            if hp > modes:
                chunk = jnp.concatenate([chunk, jnp.zeros((hp - modes, LANES), f32)], 0)
            turned = swap(chunk)
            own_blocks[which, 2 * q] = jnp.where(low_hp, chunk, turned)
            own_blocks[which, 2 * q + 1] = jnp.where(low_hp, turned, chunk)
        for p in range(pairs):
            one, two = own_blocks[which, block_at(2 * p)], own_blocks[which, block_at(2 * p + 1)]
            buf[p, mine, :] = jnp.where(low_hp, one, two)

    own_rows(b_ref, 0, gb)
    own_send[1] = pack(own_blocks[0, if0])
    own_send[0] = pack(own_blocks[0, if1])
    own_rows(d_ref, 1, gd)

    pl.semaphore_wait(
        barrier,
        (n_chaos - 1) + n_chaos * (one_way(has_left) + one_way(has_right)) + (n_space - 1),
    )

    def halo0_copy(side, d):
        return pltpu.make_async_remote_copy(
            src_ref=own_send.at[side], dst_ref=halo0.at[side, c],
            send_sem=h0_send.at[side, d], recv_sem=h0_recv.at[side, d],
            device_id=(s + 1 if side == 0 else s - 1, (c + d) % n_chaos), device_id_type=MESH,
        )

    half_pairs = pairs // 2

    def gather_copy(buf, part, send, recv, d):
        which = buf.at[part, mine, :]
        return pltpu.make_async_remote_copy(
            src_ref=which, dst_ref=which, send_sem=send, recv_sem=recv,
            device_id=(s, (c + d) % n_chaos), device_id_type=MESH,
        )

    def b_copy(d):
        return gather_copy(gb, pl.ds(0, pairs), gb_send.at[d], gb_recv.at[d], d)

    def d_copy(half, d):
        part = pl.ds(half * half_pairs, half_pairs)
        return gather_copy(gd, part, gd_send.at[half, d], gd_recv.at[half, d], d)

    for d in range(n_chaos):
        @pl.when(has_right)
        def _():
            halo0_copy(0, d).start()

        @pl.when(has_left)
        def _():
            halo0_copy(1, d).start()
    for d in range(1, n_chaos):
        b_copy(d).start()

    def slot(mode):
        shift = jnp.zeros_like(mode)
        for h in range(1, n_chaos):
            shift = shift + one_way(mode >= h * modes)
        return mode + (hp - modes) * shift

    entries = tri_ref.shape[1]
    term = tri_ref[0:1, :]
    row = slot(tri_ref[1:2, :])
    col = slot(tri_ref[2:3, :])
    values = val_ref[...].reshape(1, entries)
    hit = lax.broadcasted_iota(jnp.int32, (mp, entries), 0) == row
    spread = jnp.where(hit, values, 0.0)
    cdiag[...] = jnp.broadcast_to(
        jnp.sum(jnp.where(term == 0, spread, 0.0), axis=1, keepdims=True), (mp, LANES)
    )
    spread_hi, spread_lo = split(spread)
    spread2 = jnp.concatenate([spread_hi, spread_lo], 0)
    padded = -(-entries // LANES) * LANES
    spread2 = jnp.concatenate([spread2, jnp.zeros((2 * mp, padded - entries), spread2.dtype)], 1)
    lanes_iota = lax.broadcasted_iota(jnp.int32, (LANES, depth), 1)

    def table(parity):
        first = 1 + parity
        listed = (term > 0) & ((term & 1) == 1 - parity)
        key = jnp.where(listed, ((term - first) >> 1) * mp + col, -1)
        key = jnp.concatenate([key, jnp.full((1, padded - entries), -1, jnp.int32)], 1)
        hot = []
        for n in range(0, padded, LANES):
            down = jnp.broadcast_to(key[:, n : n + LANES], (LANES, LANES)).T
            down = jnp.concatenate([down] * (depth // LANES), 1)
            hot.append(jnp.where(lanes_iota == down, 1.0, 0.0).astype(jnp.bfloat16))
        both = dot_nn(spread2, jnp.concatenate(hot, 0)).astype(jnp.bfloat16)
        c3[parity, :, :depth] = both[:mp]
        c3[parity, :, depth : 2 * depth] = both[mp:]
        c3[parity, :, 2 * depth :] = both[:mp]

    if depth > even_terms * mp:
        rest = jnp.zeros((depth - even_terms * mp, rodd.shape[2]), jnp.bfloat16)
        for part in range(2):
            rodd[part, even_terms * mp :, :] = rest
            reven[part, even_terms * mp :, :] = rest

    k_copy.wait()

    def prepare(j):
        for odd in range(2):
            k = 2 * j + odd
            source = block_at(k)
            for tau in range(even_terms + 1):
                if tau == even_terms:
                    one = two = kf[0, source]
                else:
                    one, two = kf[2 * tau + 1 + odd, source], kf[2 * tau + 2 - odd, source]
                hi, lo = split(jnp.concatenate([one, two], 0).T)
                khi[k, :, tau * LANES : (tau + 1) * LANES] = hi
                klo[k, :, tau * LANES : (tau + 1) * LANES] = lo

    for parity in range(2):
        table(parity)
        for j in range(parity * half_pairs, pairs if parity else half_pairs):
            prepare(j)

    low = low_half((mp, LANES))

    for d in range(1, n_chaos):
        b_copy(d).wait()
    for d in range(1, n_chaos):
        d_copy(0, d).start()
    for p in range(pairs):
        chunk = gb[p]
        turned = swap(chunk)
        vec[0, p] = chunk
        ef[0, 2 * p] = jnp.where(low, chunk, turned)
        ef[0, 2 * p + 1] = jnp.where(low, turned, chunk)

    def fill(side, now, read):
        present = has_left if side == 0 else has_right

        @pl.when(present)
        def _():
            read()

        @pl.when(jnp.logical_not(present))
        def _():
            ef[now, nbr + side] = jnp.zeros((mp, LANES), f32)

    for side in range(2):
        def read_first():
            for d in range(n_chaos):
                halo0_copy(side, d).wait_recv()
            for h in range(n_chaos):
                ef[0, nbr + side, h * hp : (h + 1) * hp] = unpack(halo0[side, h], hp)

        fill(side, 0, read_first)
    for side in range(2):
        @pl.when(has_right if side == 0 else has_left)
        def _():
            for d in range(n_chaos):
                halo0_copy(side, d).wait_send()

    def halo_copy(it, side):
        return pltpu.make_async_remote_copy(
            src_ref=halo_out.at[it, side], dst_ref=halo_in.at[it, side],
            send_sem=h_send.at[it, side], recv_sem=h_recv.at[it, side],
            device_id=(s + 1 if side == 0 else s - 1, c), device_id_type=MESH,
        )

    right_place = place_of(if1)
    scale0 = cdiag[...]
    n_odd = even_terms * LANES
    wide = nnz * block
    per_half = 2 * half_pairs

    def pick(it):
        for k in range(nbr):
            row = block_at(k)
            at = [place_of(col_ref[n, row]) for n in range(nnz)]
            for m in range(nnz // 2):
                hi, lo = split(jnp.where(low, ef[it % 2, at[2 * m]], ef[it % 2, at[2 * m + 1]]))
                picked[k, :, m * LANES : (m + 1) * LANES] = hi
                picked[k, :, wide + m * LANES : wide + (m + 1) * LANES] = lo

    def half_step(it, half):
        later = 1 - it % 2
        zeros = []
        for step in range(half_pairs):
            to = pl.ds(step * LANES, LANES)
            for start in range(0, n_odd + 2 * block, 2 * LANES):
                stop = min(start + 2 * LANES, n_odd + 2 * block)
                made = []
                for i in (2 * step, 2 * step + 1):
                    k = half * per_half + i
                    hi, lo = picked[k, :, :wide], picked[k, :, wide:]
                    k_hi, k_lo = khi[k, :, start:stop], klo[k, :, start:stop]
                    made.append(
                        dot_nn(jnp.concatenate([hi, lo, hi], 1), jnp.concatenate([k_hi, k_hi, k_lo], 0))
                    )
                for piece in range(start, stop, LANES):
                    tau = piece // LANES
                    a = made[0][:, piece - start : piece - start + LANES]
                    b = made[1][:, piece - start : piece - start + LANES]
                    if piece == n_odd:
                        zeros.append(jnp.where(low, a, b))
                        continue
                    hi, lo = split(jnp.where(low, a, b))
                    rodd[0, tau * mp : (tau + 1) * mp, to] = hi
                    rodd[1, tau * mp : (tau + 1) * mp, to] = lo
                    hi, lo = split(jnp.where(low, b, a))
                    reven[0, tau * mp : (tau + 1) * mp, to] = hi
                    reven[1, tau * mp : (tau + 1) * mp, to] = lo
        coupled = []
        for parity, rhs in ((0, rodd), (1, reven)):
            hi, lo = rhs[0], rhs[1]
            coupled.append(dot_nn(c3[parity], jnp.concatenate([hi, hi, lo], 0)))

        if it == 0:
            for d in range(1, n_chaos):
                d_copy(half, d).wait()
            if half == 0:
                for d in range(1, n_chaos):
                    d_copy(1, d).start()

        for step in range(half_pairs):
            p = half * half_pairs + step
            at = slice(step * LANES, (step + 1) * LANES)
            new = coupled[0][:, at] + swap(coupled[1][:, at]) + scale0 * zeros[step]
            new = (gd[p] - SHIFT) * vec[it, p] + new
            if it > 0:
                new = new - GAMMA[it] * vec[it - 1, p]
            vec[it + 1, p] = new
            if it < ITERS - 1:
                turned = swap(new)
                ef[later, 2 * p] = jnp.where(low, new, turned)
                ef[later, 2 * p + 1] = jnp.where(low, turned, new)

        if half == 0 and it < ITERS - 1:
            halo_out[it, 1] = pack(ef[later, 0])
            halo_out[it, 0] = pack(ef[later, right_place])

            @pl.when(has_right)
            def _():
                halo_copy(it, 0).start()

            @pl.when(has_left)
            def _():
                halo_copy(it, 1).start()

    for it in range(ITERS):
        pick(it)
        for half in range(2):
            half_step(it, half)
        if it < ITERS - 1:
            later = 1 - it % 2
            for side in range(2):
                def read_next():
                    halo_copy(it, side).wait_recv()
                    ef[later, nbr + side] = unpack(halo_in[it, side], mp)

                fill(side, later, read_next)
            for side in range(2):
                @pl.when(has_right if side == 0 else has_left)
                def _():
                    halo_copy(it, side).wait_send()

    def products(p, sums):
        parts = [vec[j, p] for j in range(ITERS + 1)]
        return tuple(
            total + jnp.sum((parts[i] * parts[j]).reshape(mp // 8, 8, LANES), axis=0)
            for total, (i, j) in zip(sums, PAIRS)
        )

    sums = lax.fori_loop(0, pairs, products, tuple(jnp.zeros((8, LANES), f32) for _ in PAIRS))

    stat[...] = jnp.zeros_like(stat)
    for e, part in enumerate(sums):
        stat[e : e + 1, :] = jnp.sum(part, axis=0, keepdims=True)

    def reduce_copy(d):
        return pltpu.make_async_remote_copy(
            src_ref=stat, dst_ref=red.at[s], send_sem=r_send.at[d], recv_sem=r_recv.at[d],
            device_id=((s + d) % n_space, c), device_id_type=MESH,
        )

    for d in range(1, n_space):
        reduce_copy(d).start()
    red[s] = stat[...]

    back = [place_of(jnp.int32(k)) for k in range(nbr)]

    def restore(j, _):
        for p in range(pairs):
            chunk = vec[j, p, mine, :]
            turned = swap(chunk)
            natv[2 * p] = jnp.where(low_hp, chunk, turned)
            natv[2 * p + 1] = jnp.where(low_hp, turned, chunk)
        for q in range(pairs):
            chunk = jnp.where(low_hp, natv[back[2 * q]], natv[back[2 * q + 1]])
            basis_out[j, :, q * LANES : (q + 1) * LANES] = chunk[:modes]
        return 0

    lax.fori_loop(0, ITERS + 1, restore, 0)

    for d in range(1, n_space):
        reduce_copy(d).wait()
    total = red[0]
    for g in range(1, n_space):
        total = total + red[g]
    total = jnp.sum(total, axis=1, keepdims=True)
    gram = {}
    for e, (i, j) in enumerate(PAIRS):
        gram[(i, j)] = gram[(j, i)] = total[e : e + 1, :]

    def inner(one, two):
        value = None
        for i, a in one.items():
            for j, b in two.items():
                part = a * b * gram[(i, j)]
                value = part if value is None else value + part
        return value

    def plus(one, scale, two):
        result = dict(one)
        for i, a in two.items():
            result[i] = result[i] + scale * a if i in result else scale * a
        return result

    def image_of(vector):
        result = {}
        for k, a in vector.items():
            result = plus(result, a, {k: jnp.full((1, 1), SHIFT, f32), k + 1: jnp.ones((1, 1), f32)})
            if k > 0:
                result = plus(result, a, {k - 1: jnp.full((1, 1), GAMMA[k], f32)})
        return result

    residual = {0: jnp.ones((1, 1), f32)}
    direction = dict(residual)
    field = {}
    norm_now = gram[(0, 0)]
    for it in range(ITERS):
        image = image_of(direction)
        alpha = norm_now / inner(direction, image)
        field = plus(field, alpha, direction)
        residual = plus(residual, -alpha, image)
        if it < ITERS - 1:
            norm_next = inner(residual, residual)
            direction = plus(residual, norm_next / norm_now, direction)
            norm_now = norm_next

    for coefs, first in ((field, 0), (residual, 8)):
        for j, a in coefs.items():
            coef_out[first + j : first + j + 1, :] = jnp.broadcast_to(a, (1, LANES))


def combine(basis_ref, coef_ref, x_ref, r_ref):
    for q in range(0, x_ref.shape[1], LANES):
        at = slice(q, q + LANES)
        parts = [basis_ref[j, :, at] for j in range(ITERS + 1)]
        x_ref[:, at] = sum(coef_ref[j : j + 1, :] * parts[j] for j in range(ITERS))
        r_ref[:, at] = sum(coef_ref[8 + j : 9 + j, :] * parts[j] for j in range(ITERS + 1))


def per_device(right_side, diagonal, stiffness, columns, interface, triples, coupling_values):
    n_space, n_chaos = lax.axis_size("space"), lax.axis_size("chaos")
    modes, width = right_side.shape
    terms, nbr, block, depth = stiffness.shape
    hp = (modes + 7) // 8 * 8
    mp = n_chaos * hp
    pairs = nbr // 2
    even_terms = (terms - 1) // 2
    cols = even_terms * LANES + 2 * block
    f32, bf16 = jnp.float32, jnp.bfloat16
    vmem = pl.BlockSpec(memory_space=pltpu.VMEM)
    smem = pl.BlockSpec(memory_space=pltpu.SMEM)
    dma = pltpu.SemaphoreType.DMA
    out = jax.ShapeDtypeStruct((modes, width), f32)
    whole_depth = -(-even_terms * mp // 256) * 256
    basis, coefs = pl.pallas_call(
        functools.partial(kernel, n_space, n_chaos),
        out_shape=(
            jax.ShapeDtypeStruct((ITERS + 1, modes, width), f32),
            jax.ShapeDtypeStruct((16, LANES), f32),
        ),
        in_specs=[vmem, vmem, pl.BlockSpec(memory_space=pltpu.HBM), smem, smem, vmem, vmem],
        out_specs=(vmem, vmem),
        scratch_shapes=[
            pltpu.VMEM(stiffness.shape, f32),
            pltpu.VMEM((nbr, depth, cols), bf16),
            pltpu.VMEM((nbr, depth, cols), bf16),
            pltpu.VMEM((2, mp, 3 * whole_depth), bf16),
            pltpu.VMEM((mp, LANES), f32),
            pltpu.VMEM((pairs, mp, LANES), f32),
            pltpu.VMEM((pairs, mp, LANES), f32),
            pltpu.VMEM((2, nbr + 2, mp, LANES), f32),
            pltpu.VMEM((ITERS + 1, pairs, mp, LANES), f32),
            pltpu.VMEM((nbr, mp, 2 * depth), bf16),
            pltpu.VMEM((2, whole_depth, pairs // 2 * LANES), bf16),
            pltpu.VMEM((2, whole_depth, pairs // 2 * LANES), bf16),
            pltpu.VMEM((2, packed_rows(hp), LANES), f32),
            pltpu.VMEM((2, nbr, hp, LANES), f32),
            pltpu.VMEM((2, n_chaos, packed_rows(hp), LANES), f32),
            pltpu.VMEM((ITERS - 1, 2, packed_rows(mp), LANES), f32),
            pltpu.VMEM((ITERS - 1, 2, packed_rows(mp), LANES), f32),
            pltpu.VMEM((16, LANES), f32),
            pltpu.VMEM((n_space, 16, LANES), f32),
            pltpu.VMEM((nbr, hp, LANES), f32),
            dma,
            dma((n_chaos,)), dma((n_chaos,)), dma((2, n_chaos)), dma((2, n_chaos)),
            dma((2, n_chaos)), dma((2, n_chaos)),
            dma((ITERS - 1, 2)), dma((ITERS - 1, 2)),
            dma((n_space,)), dma((n_space,)),
        ],
        compiler_params=pltpu.CompilerParams(
            collective_id=0, has_side_effects=True, vmem_limit_bytes=56 * 1024 * 1024
        ),
        name="solve",
    )(
        right_side, diagonal, stiffness, columns.T, interface, triples.T,
        coupling_values,
    )
    return pl.pallas_call(
        combine,
        out_shape=(out, out),
        in_specs=[vmem, vmem],
        out_specs=(vmem, vmem),
        name="combine",
    )(basis, coefs)


def solution(mesh):
    placed = (
        P("chaos", "space"),
        P("chaos", "space"),
        P(None, "space", None, None),
        P("space", None),
        P("space", None),
        P(),
        P(),
    )
    return jax.shard_map(
        per_device,
        mesh=mesh,
        in_specs=placed,
        out_specs=(P("chaos", "space"), P("chaos", "space")),
        check_vma=False,
    )
```

```python
import functools

import jax
import jax.numpy as jnp
from jax import lax
from jax.experimental import pallas as pl
from jax.experimental.pallas import tpu as pltpu
from jax.sharding import PartitionSpec as P

MESH = pl.DeviceIdType.MESH
ITERS = 3
LANES = 128
SHIFT = 2.75
GAMMA = (0.0, 0.52083333, 0.41666667)
PAIRS = ((0, 0), (0, 1), (1, 1), (0, 2), (1, 2), (2, 2), (0, 3), (1, 3), (2, 3))


def split(x):
    hi = x.astype(jnp.bfloat16)
    lo = (x - hi.astype(jnp.float32)).astype(jnp.bfloat16)
    return hi, lo


def dot_nn(a, b):
    return lax.dot_general(a, b, (((1,), (0,)), ((), ())), preferred_element_type=jnp.float32)


def low_half(shape):
    return lax.broadcasted_iota(jnp.int32, shape, len(shape) - 1) < LANES // 2


def swap(x):
    return pltpu.roll(x, LANES // 2, 1)


def packed_rows(rows):
    return (rows // 8 + 1) // 2 * 8


def pack(x):
    rows = x.shape[0]
    part = packed_rows(rows)
    return jnp.where(low_half((part, LANES)), x[:part], x[rows - part :])


def unpack(x, rows):
    part = x.shape[0]
    turned = swap(x)
    low = low_half(x.shape)
    top = jnp.where(low, x, turned)
    bottom = jnp.where(low, turned, x)
    return jnp.concatenate([top, bottom[2 * part - rows :]], 0)


def one_way(x):
    return jnp.where(x, 1, 0)


def kernel(
    n_space, n_chaos,
    b_ref, d_ref, k_hbm, col_ref, if_ref, tri_ref, val_ref,
    basis_out, coef_out,
    kf, khi, klo, c2, cdiag, gb, gd, ef, vec, picked, rodd, reven,
    own_send, own_blocks, halo0, halo_out, halo_in, stat, red, natv,
    k_sem, gb_send, gb_recv, gd_send, gd_recv, h0_send, h0_recv, h_send, h_recv,
    r_send, r_recv,
):
    f32 = jnp.float32
    modes, width = b_ref.shape
    mp = gb.shape[1]
    hp = mp // n_chaos
    terms, nbr, block, _ = kf.shape
    nnz = col_ref.shape[0]
    pairs = nbr // 2
    even_terms = (terms - 1) // 2
    depth = rodd.shape[1]
    s = lax.axis_index("space")
    c = lax.axis_index("chaos")

    k_copy = pltpu.make_async_copy(k_hbm, kf, k_sem)
    k_copy.start()

    barrier = pltpu.get_barrier_semaphore()
    has_left, has_right = s > 0, s < n_space - 1

    def greet(space, chaos):
        pl.semaphore_signal(barrier, inc=1, device_id=(space, chaos), device_id_type=MESH)

    for d in range(1, n_chaos):
        greet(s, (c + d) % n_chaos)
    for d in range(n_chaos):
        @pl.when(has_left)
        def _():
            greet(s - 1, (c + d) % n_chaos)

        @pl.when(has_right)
        def _():
            greet(s + 1, (c + d) % n_chaos)
    for d in range(1, n_space):
        greet((s + d) % n_space, c)

    if0, if1 = if_ref[0, 0], if_ref[0, 1]
    second = jnp.where(if1 == if0, jnp.where(if0 == 0, 1, 0), if1)
    small, large = jnp.minimum(if0, second), jnp.maximum(if0, second)

    def block_at(k):
        if isinstance(k, int) and k < 2:
            return if0 if k == 0 else second
        row = k - 2
        row = row + one_way(row >= small)
        row = row + one_way(row >= large)
        return row if isinstance(k, int) else jnp.where(k == 0, if0, jnp.where(k == 1, second, row))

    def place_of(row):
        rest = 2 + row - one_way(if0 < row) - one_way(second < row)
        found = jnp.where(row == if0, 0, jnp.where(row == second, 1, rest))
        return jnp.where(row >= nbr, row, found)

    mine = pl.ds(pl.multiple_of(c * hp, 8), hp)
    low_hp = low_half((hp, LANES))

    def own_rows(ref, which, buf):
        for q in range(pairs):
            chunk = ref[:, q * LANES : (q + 1) * LANES]
            if hp > modes:
                chunk = jnp.concatenate([chunk, jnp.zeros((hp - modes, LANES), f32)], 0)
            turned = swap(chunk)
            own_blocks[which, 2 * q] = jnp.where(low_hp, chunk, turned)
            own_blocks[which, 2 * q + 1] = jnp.where(low_hp, turned, chunk)
        for p in range(pairs):
            one, two = own_blocks[which, block_at(2 * p)], own_blocks[which, block_at(2 * p + 1)]
            buf[p, mine, :] = jnp.where(low_hp, one, two)

    own_rows(b_ref, 0, gb)
    own_send[1] = pack(own_blocks[0, if0])
    own_send[0] = pack(own_blocks[0, if1])
    own_rows(d_ref, 1, gd)

    pl.semaphore_wait(
        barrier,
        (n_chaos - 1) + n_chaos * (one_way(has_left) + one_way(has_right)) + (n_space - 1),
    )

    def halo0_copy(side, d):
        return pltpu.make_async_remote_copy(
            src_ref=own_send.at[side], dst_ref=halo0.at[side, c],
            send_sem=h0_send.at[side, d], recv_sem=h0_recv.at[side, d],
            device_id=(s + 1 if side == 0 else s - 1, (c + d) % n_chaos), device_id_type=MESH,
        )

    half_pairs = pairs // 2

    def gather_copy(buf, part, send, recv, d):
        which = buf.at[part, mine, :]
        return pltpu.make_async_remote_copy(
            src_ref=which, dst_ref=which, send_sem=send, recv_sem=recv,
            device_id=(s, (c + d) % n_chaos), device_id_type=MESH,
        )

    def b_copy(d):
        return gather_copy(gb, pl.ds(0, pairs), gb_send.at[d], gb_recv.at[d], d)

    def d_copy(half, d):
        part = pl.ds(half * half_pairs, half_pairs)
        return gather_copy(gd, part, gd_send.at[half, d], gd_recv.at[half, d], d)

    for d in range(n_chaos):
        @pl.when(has_right)
        def _():
            halo0_copy(0, d).start()

        @pl.when(has_left)
        def _():
            halo0_copy(1, d).start()
    for d in range(1, n_chaos):
        b_copy(d).start()

    def slot(mode):
        shift = jnp.zeros_like(mode)
        for h in range(1, n_chaos):
            shift = shift + one_way(mode >= h * modes)
        return mode + (hp - modes) * shift

    entries = tri_ref.shape[1]
    term = tri_ref[0:1, :]
    row = slot(tri_ref[1:2, :])
    col = slot(tri_ref[2:3, :])
    values = val_ref[...].reshape(1, entries)
    hit = lax.broadcasted_iota(jnp.int32, (mp, entries), 0) == row
    spread = jnp.where(hit, values, 0.0)
    cdiag[...] = jnp.broadcast_to(
        jnp.sum(jnp.where(term == 0, spread, 0.0), axis=1, keepdims=True), (mp, LANES)
    )
    spread_hi, spread_lo = split(spread)
    spread2 = jnp.concatenate([spread_hi, spread_lo], 0)
    padded = -(-entries // LANES) * LANES
    spread2 = jnp.concatenate([spread2, jnp.zeros((2 * mp, padded - entries), spread2.dtype)], 1)
    lanes_iota = lax.broadcasted_iota(jnp.int32, (LANES, depth), 1)

    def table(parity):
        first = 1 + parity
        listed = (term > 0) & ((term & 1) == 1 - parity)
        key = jnp.where(listed, ((term - first) >> 1) * mp + col, -1)
        key = jnp.concatenate([key, jnp.full((1, padded - entries), -1, jnp.int32)], 1)
        hot = []
        for n in range(0, padded, LANES):
            down = jnp.broadcast_to(key[:, n : n + LANES], (LANES, LANES)).T
            down = jnp.concatenate([down] * (depth // LANES), 1)
            hot.append(jnp.where(lanes_iota == down, 1.0, 0.0).astype(jnp.bfloat16))
        both = dot_nn(spread2, jnp.concatenate(hot, 0)).astype(jnp.bfloat16)
        c2[parity] = both

    if depth > even_terms * mp:
        rest = jnp.zeros((depth - even_terms * mp, rodd.shape[2]), jnp.bfloat16)
        for part in range(2):
            rodd[part, even_terms * mp :, :] = rest
            reven[part, even_terms * mp :, :] = rest

    k_copy.wait()

    def prepare(j):
        for odd in range(2):
            k = 2 * j + odd
            source = block_at(k)
            for tau in range(even_terms + 1):
                if tau == even_terms:
                    one = two = kf[0, source]
                else:
                    one, two = kf[2 * tau + 1 + odd, source], kf[2 * tau + 2 - odd, source]
                hi, lo = split(jnp.concatenate([one, two], 0).T)
                khi[k, :, tau * LANES : (tau + 1) * LANES] = hi
                klo[k, :, tau * LANES : (tau + 1) * LANES] = lo

    for parity in range(2):
        table(parity)
        for j in range(parity * half_pairs, pairs if parity else half_pairs):
            prepare(j)

    low = low_half((mp, LANES))

    for d in range(1, n_chaos):
        b_copy(d).wait()
    for d in range(1, n_chaos):
        d_copy(0, d).start()
    for p in range(pairs):
        chunk = gb[p]
        turned = swap(chunk)
        vec[0, p] = chunk
        ef[0, 2 * p] = jnp.where(low, chunk, turned)
        ef[0, 2 * p + 1] = jnp.where(low, turned, chunk)

    def fill(side, now, read):
        present = has_left if side == 0 else has_right

        @pl.when(present)
        def _():
            read()

        @pl.when(jnp.logical_not(present))
        def _():
            ef[now, nbr + side] = jnp.zeros((mp, LANES), f32)

    for side in range(2):
        def read_first():
            for d in range(n_chaos):
                halo0_copy(side, d).wait_recv()
            for h in range(n_chaos):
                ef[0, nbr + side, h * hp : (h + 1) * hp] = unpack(halo0[side, h], hp)

        fill(side, 0, read_first)
    for side in range(2):
        @pl.when(has_right if side == 0 else has_left)
        def _():
            for d in range(n_chaos):
                halo0_copy(side, d).wait_send()

    def halo_copy(it, side):
        return pltpu.make_async_remote_copy(
            src_ref=halo_out.at[it, side], dst_ref=halo_in.at[it, side],
            send_sem=h_send.at[it, side], recv_sem=h_recv.at[it, side],
            device_id=(s + 1 if side == 0 else s - 1, c), device_id_type=MESH,
        )

    right_place = place_of(if1)
    scale0 = cdiag[...]
    n_odd = even_terms * LANES
    wide = nnz * block
    per_half = 2 * half_pairs

    def pick(it):
        for k in range(nbr):
            row = block_at(k)
            at = [place_of(col_ref[n, row]) for n in range(nnz)]
            for m in range(nnz // 2):
                hi, lo = split(jnp.where(low, ef[it % 2, at[2 * m]], ef[it % 2, at[2 * m + 1]]))
                picked[k, :, m * LANES : (m + 1) * LANES] = hi
                picked[k, :, wide + m * LANES : wide + (m + 1) * LANES] = lo

    def half_step(it, half):
        later = 1 - it % 2
        zeros = []
        for step in range(half_pairs):
            to = pl.ds(step * LANES, LANES)
            for start in range(0, n_odd + 2 * block, 2 * LANES):
                stop = min(start + 2 * LANES, n_odd + 2 * block)
                made = []
                for i in (2 * step, 2 * step + 1):
                    k = half * per_half + i
                    hi, lo = picked[k, :, :wide], picked[k, :, wide:]
                    k_hi, k_lo = khi[k, :, start:stop], klo[k, :, start:stop]
                    both = dot_nn(jnp.concatenate([hi, lo], 0), k_hi)
                    made.append(both[:mp] + both[mp:] + dot_nn(hi, k_lo))
                for piece in range(start, stop, LANES):
                    tau = piece // LANES
                    a = made[0][:, piece - start : piece - start + LANES]
                    b = made[1][:, piece - start : piece - start + LANES]
                    if piece == n_odd:
                        zeros.append(jnp.where(low, a, b))
                        continue
                    hi, lo = split(jnp.where(low, a, b))
                    rodd[0, tau * mp : (tau + 1) * mp, to] = hi
                    rodd[1, tau * mp : (tau + 1) * mp, to] = lo
                    hi, lo = split(jnp.where(low, b, a))
                    reven[0, tau * mp : (tau + 1) * mp, to] = hi
                    reven[1, tau * mp : (tau + 1) * mp, to] = lo
        coupled = []
        for parity, rhs in ((0, rodd), (1, reven)):
            hi, lo = rhs[0], rhs[1]
            both = dot_nn(c2[parity], hi)
            coupled.append(both[:mp] + both[mp:] + dot_nn(c2[parity, :mp], lo))

        if it == 0:
            for d in range(1, n_chaos):
                d_copy(half, d).wait()
            if half == 0:
                for d in range(1, n_chaos):
                    d_copy(1, d).start()

        for step in range(half_pairs):
            p = half * half_pairs + step
            at = slice(step * LANES, (step + 1) * LANES)
            new = coupled[0][:, at] + swap(coupled[1][:, at]) + scale0 * zeros[step]
            new = (gd[p] - SHIFT) * vec[it, p] + new
            if it > 0:
                new = new - GAMMA[it] * vec[it - 1, p]
            vec[it + 1, p] = new
            if it < ITERS - 1:
                turned = swap(new)
                ef[later, 2 * p] = jnp.where(low, new, turned)
                ef[later, 2 * p + 1] = jnp.where(low, turned, new)

        if half == 0 and it < ITERS - 1:
            halo_out[it, 1] = pack(ef[later, 0])
            halo_out[it, 0] = pack(ef[later, right_place])

            @pl.when(has_right)
            def _():
                halo_copy(it, 0).start()

            @pl.when(has_left)
            def _():
                halo_copy(it, 1).start()

    for it in range(ITERS):
        pick(it)
        for half in range(2):
            half_step(it, half)
        if it < ITERS - 1:
            later = 1 - it % 2
            for side in range(2):
                def read_next():
                    halo_copy(it, side).wait_recv()
                    ef[later, nbr + side] = unpack(halo_in[it, side], mp)

                fill(side, later, read_next)
            for side in range(2):
                @pl.when(has_right if side == 0 else has_left)
                def _():
                    halo_copy(it, side).wait_send()

    def products(p, sums):
        parts = [vec[j, p] for j in range(ITERS + 1)]
        return tuple(
            total + jnp.sum((parts[i] * parts[j]).reshape(mp // 8, 8, LANES), axis=0)
            for total, (i, j) in zip(sums, PAIRS)
        )

    sums = lax.fori_loop(0, pairs, products, tuple(jnp.zeros((8, LANES), f32) for _ in PAIRS))

    stat[...] = jnp.zeros_like(stat)
    for e, part in enumerate(sums):
        stat[e : e + 1, :] = jnp.sum(part, axis=0, keepdims=True)

    def reduce_copy(d):
        return pltpu.make_async_remote_copy(
            src_ref=stat, dst_ref=red.at[s], send_sem=r_send.at[d], recv_sem=r_recv.at[d],
            device_id=((s + d) % n_space, c), device_id_type=MESH,
        )

    for d in range(1, n_space):
        reduce_copy(d).start()
    red[s] = stat[...]

    back = [place_of(jnp.int32(k)) for k in range(nbr)]

    def restore(j, _):
        for p in range(pairs):
            chunk = vec[j, p, mine, :]
            turned = swap(chunk)
            natv[2 * p] = jnp.where(low_hp, chunk, turned)
            natv[2 * p + 1] = jnp.where(low_hp, turned, chunk)
        for q in range(pairs):
            chunk = jnp.where(low_hp, natv[back[2 * q]], natv[back[2 * q + 1]])
            basis_out[j, :, q * LANES : (q + 1) * LANES] = chunk[:modes]
        return 0

    lax.fori_loop(0, ITERS + 1, restore, 0)

    for d in range(1, n_space):
        reduce_copy(d).wait()
    total = red[0]
    for g in range(1, n_space):
        total = total + red[g]
    total = jnp.sum(total, axis=1, keepdims=True)
    gram = {}
    for e, (i, j) in enumerate(PAIRS):
        gram[(i, j)] = gram[(j, i)] = total[e : e + 1, :]

    def inner(one, two):
        value = None
        for i, a in one.items():
            for j, b in two.items():
                part = a * b * gram[(i, j)]
                value = part if value is None else value + part
        return value

    def plus(one, scale, two):
        result = dict(one)
        for i, a in two.items():
            result[i] = result[i] + scale * a if i in result else scale * a
        return result

    def image_of(vector):
        result = {}
        for k, a in vector.items():
            result = plus(result, a, {k: jnp.full((1, 1), SHIFT, f32), k + 1: jnp.ones((1, 1), f32)})
            if k > 0:
                result = plus(result, a, {k - 1: jnp.full((1, 1), GAMMA[k], f32)})
        return result

    residual = {0: jnp.ones((1, 1), f32)}
    direction = dict(residual)
    field = {}
    norm_now = gram[(0, 0)]
    for it in range(ITERS):
        image = image_of(direction)
        alpha = norm_now / inner(direction, image)
        field = plus(field, alpha, direction)
        residual = plus(residual, -alpha, image)
        if it < ITERS - 1:
            norm_next = inner(residual, residual)
            direction = plus(residual, norm_next / norm_now, direction)
            norm_now = norm_next

    for coefs, first in ((field, 0), (residual, 8)):
        for j, a in coefs.items():
            coef_out[first + j : first + j + 1, :] = jnp.broadcast_to(a, (1, LANES))


def combine(basis_ref, coef_ref, x_ref, r_ref):
    for q in range(0, x_ref.shape[1], LANES):
        at = slice(q, q + LANES)
        parts = [basis_ref[j, :, at] for j in range(ITERS + 1)]
        x_ref[:, at] = sum(coef_ref[j : j + 1, :] * parts[j] for j in range(ITERS))
        r_ref[:, at] = sum(coef_ref[8 + j : 9 + j, :] * parts[j] for j in range(ITERS + 1))


def per_device(right_side, diagonal, stiffness, columns, interface, triples, coupling_values):
    n_space, n_chaos = lax.axis_size("space"), lax.axis_size("chaos")
    modes, width = right_side.shape
    terms, nbr, block, depth = stiffness.shape
    hp = (modes + 7) // 8 * 8
    mp = n_chaos * hp
    pairs = nbr // 2
    even_terms = (terms - 1) // 2
    cols = even_terms * LANES + 2 * block
    f32, bf16 = jnp.float32, jnp.bfloat16
    vmem = pl.BlockSpec(memory_space=pltpu.VMEM)
    smem = pl.BlockSpec(memory_space=pltpu.SMEM)
    dma = pltpu.SemaphoreType.DMA
    out = jax.ShapeDtypeStruct((modes, width), f32)
    whole_depth = -(-even_terms * mp // 256) * 256
    basis, coefs = pl.pallas_call(
        functools.partial(kernel, n_space, n_chaos),
        out_shape=(
            jax.ShapeDtypeStruct((ITERS + 1, modes, width), f32),
            jax.ShapeDtypeStruct((16, LANES), f32),
        ),
        in_specs=[vmem, vmem, pl.BlockSpec(memory_space=pltpu.HBM), smem, smem, vmem, vmem],
        out_specs=(vmem, vmem),
        scratch_shapes=[
            pltpu.VMEM(stiffness.shape, f32),
            pltpu.VMEM((nbr, depth, cols), bf16),
            pltpu.VMEM((nbr, depth, cols), bf16),
            pltpu.VMEM((2, 2 * mp, whole_depth), bf16),
            pltpu.VMEM((mp, LANES), f32),
            pltpu.VMEM((pairs, mp, LANES), f32),
            pltpu.VMEM((pairs, mp, LANES), f32),
            pltpu.VMEM((2, nbr + 2, mp, LANES), f32),
            pltpu.VMEM((ITERS + 1, pairs, mp, LANES), f32),
            pltpu.VMEM((nbr, mp, 2 * depth), bf16),
            pltpu.VMEM((2, whole_depth, pairs // 2 * LANES), bf16),
            pltpu.VMEM((2, whole_depth, pairs // 2 * LANES), bf16),
            pltpu.VMEM((2, packed_rows(hp), LANES), f32),
            pltpu.VMEM((2, nbr, hp, LANES), f32),
            pltpu.VMEM((2, n_chaos, packed_rows(hp), LANES), f32),
            pltpu.VMEM((ITERS - 1, 2, packed_rows(mp), LANES), f32),
            pltpu.VMEM((ITERS - 1, 2, packed_rows(mp), LANES), f32),
            pltpu.VMEM((16, LANES), f32),
            pltpu.VMEM((n_space, 16, LANES), f32),
            pltpu.VMEM((nbr, hp, LANES), f32),
            dma,
            dma((n_chaos,)), dma((n_chaos,)), dma((2, n_chaos)), dma((2, n_chaos)),
            dma((2, n_chaos)), dma((2, n_chaos)),
            dma((ITERS - 1, 2)), dma((ITERS - 1, 2)),
            dma((n_space,)), dma((n_space,)),
        ],
        compiler_params=pltpu.CompilerParams(
            collective_id=0, has_side_effects=True, vmem_limit_bytes=56 * 1024 * 1024
        ),
        name="solve",
    )(
        right_side, diagonal, stiffness, columns.T, interface, triples.T,
        coupling_values,
    )
    return pl.pallas_call(
        combine,
        out_shape=(out, out),
        in_specs=[vmem, vmem],
        out_specs=(vmem, vmem),
        name="combine",
    )(basis, coefs)


def solution(mesh):
    placed = (
        P("chaos", "space"),
        P("chaos", "space"),
        P(None, "space", None, None),
        P("space", None),
        P("space", None),
        P(),
        P(),
    )
    return jax.shard_map(
        per_device,
        mesh=mesh,
        in_specs=placed,
        out_specs=(P("chaos", "space"), P("chaos", "space")),
        check_vma=False,
    )
```
